512 devices in a mesh: orient: 128 (over z, x, core), dom: 4 (over y).
Axes of the slice: x: 4, y: 4, z: 16, core: 2. Of those that a mesh axis runs over, the one named last changes fastest.
Arguments:
- images: bfloat16 [1152, 2, 2048], P('dom'), may hold values from -9 to 9
- references: bfloat16 [4608, 2, 2048], P('orient'), may hold values from -3 to 3
- noise_weights: float32 [64, 2048], replicated, may hold values from 0.01 to 0.1
- log_prior: float32 [8, 16], replicated, may hold values from -6 to 6
- groups: int32 [1152], P('dom'), may hold values from 0 to 63
- prior_index: int32 [1152], P('dom'), may hold values from 0 to 7
- class_map: int32 [4608], P('orient'), may hold values from 0 to 15, as said below
Outputs:
- new_references: float32 [4608, 2, 2048], P('orient', None, 'dom')
- log_likelihood: float32 [1152], P('dom')
The draws below stay inside these ranges and needn't reach their ends.
Inputs may be any that keep to these rules, and one draw needn't show every extreme that they name: `class_map`: each class owns one run of 288 consecutive orientations, a different class for each run.
All inputs are finite; a program needn't handle non-finite values.
Results may differ from the reference program's by a relative error of at most 0.0084.
Values sent between devices are 32-bit elements; how exact they have to be, the bound alone decides.
No kernel may reach another device: no remote copies, remote signals or barrier semaphores. Data moves between devices by JAX's collectives and lax.ppermute only.
A program may use at most 64 MiB of HBM per device.

```python
import math
import jax
import jax.numpy as jnp
from jax import lax

BOX = 64
HALF = 2048
SHIFTS = 9
CLASSES = 16
NGROUPS = 64
PRIOR_TABLES = 8
ORI_DEV = 36
ORIENTS = 4608
PARTICLES = 1152
N_ORIENT = 128


aligned_count = 8


def shared_references(key):
    base_key = jax.random.fold_in(key, 101)
    ref_values = jnp.clip(0.5 * jax.random.normal(base_key, (ORIENTS, 2, HALF), jnp.float32), -3.0, 3.0)
    return ref_values


def drawn_pairs(key):
    first_orient = jax.random.randint(jax.random.fold_in(key, 202), (aligned_count,), 0, ORIENTS // 2)
    return (first_orient, first_orient + ORIENTS // 2)


def draw_references(key, part):
    ref_values = shared_references(key)
    first_orient, second_orient = drawn_pairs(key)
    ref_values = ref_values.at[second_orient].set(0.995 * ref_values[first_orient])
    return ref_values.astype(jnp.bfloat16)


def draw_images(key, part):
    noise_key = jax.random.fold_in(key, 303)
    image_values = jnp.clip(jax.random.normal(noise_key, (PARTICLES, 2, HALF), jnp.float32), -6.0, 6.0)
    first_orient, second_orient = drawn_pairs(key)
    ref_values = jnp.clip(shared_references(key)[first_orient], -1.0, 1.0)
    aligned_rows = jnp.arange(aligned_count, dtype=jnp.int32) * (PARTICLES // aligned_count)
    strength = jnp.array([3.5, 5.0, 7.0, 9.0], jnp.float32)[jnp.arange(aligned_count) % 4]
    image_values = image_values.at[aligned_rows].set(strength[:, None, None] * ref_values)
    return image_values.astype(jnp.bfloat16)


def draw_class_map(key, part):
    class_order = jax.random.permutation(jax.random.fold_in(key, 404), CLASSES)
    run_length = ORIENTS // CLASSES
    return class_order[jnp.arange(ORIENTS, dtype=jnp.int32) // run_length].astype(jnp.int32)


def place_ends(result, key, low, top_value):
    shape = result.shape
    index_at = [jax.random.randint(jax.random.fold_in(key, axis), (), 0, shape[axis]) for axis in range(len(shape))]
    result = result.at[tuple(index_at)].set(low)
    longest = shape.index(max(shape))
    index_at[longest] = (index_at[longest] + 1) % shape[longest]
    return result.at[tuple(index_at)].set(top_value)


def normal_values(stream_key, dims, deviation, reach, kind=jnp.bfloat16):
    return jnp.clip(deviation * jax.random.normal(stream_key, dims, jnp.float32), -reach, reach).astype(kind)


def setup_inputs(seed: int = 0) -> dict:
    keys = jax.random.split(jax.random.key(seed), 8)
    images = draw_images(jax.random.fold_in(keys[7], 71), 0)
    references = draw_references(jax.random.fold_in(keys[7], 71), 0)
    noise_weights = jnp.clip(jnp.exp(jax.random.uniform(keys[2], (NGROUPS, HALF), jnp.float32, math.log(0.01), math.log(0.1))), 0.01, 0.1)
    log_prior = normal_values(keys[3], (PRIOR_TABLES, CLASSES), 1.5, 6.0, jnp.float32)
    groups = place_ends(jax.random.randint(keys[4], (PARTICLES,), 0, NGROUPS), jax.random.fold_in(keys[4], 1), 0, NGROUPS - 1).astype(jnp.int32)
    prior_index = place_ends(jax.random.randint(keys[5], (PARTICLES,), 0, PRIOR_TABLES), jax.random.fold_in(keys[5], 1), 0, PRIOR_TABLES - 1).astype(jnp.int32)
    class_map = draw_class_map(jax.random.fold_in(keys[7], 71), 0)
    return {"images": images, "references": references, "noise_weights": noise_weights, "log_prior": log_prior, "groups": groups, "prior_index": prior_index, "class_map": class_map}


ridge = 0.01


def phase_tables(coeffs):
    coef_index = jnp.arange(coeffs, dtype=jnp.int32)
    row_id = coef_index // (BOX // 2)
    freq_y = (row_id + BOX // 2) % BOX - BOX // 2
    freq_x = coef_index % (BOX // 2)
    shift_id = jnp.arange(SHIFTS, dtype=jnp.int32)
    move_x = shift_id % 3 - 1
    move_y = shift_id // 3 - 1
    phase_angle = (move_x[:, None] * freq_x[None, :] + move_y[:, None] * freq_y[None, :]).astype(jnp.float32) * (2.0 * jnp.pi / BOX)
    return jnp.cos(phase_angle), jnp.sin(phase_angle)


def shift_references(ref_wide, phase_cos, phase_sin):
    real_part = ref_wide[:, None, 0, :] * phase_cos[None] + ref_wide[:, None, 1, :] * phase_sin[None]
    imag_part = ref_wide[:, None, 1, :] * phase_cos[None] - ref_wide[:, None, 0, :] * phase_sin[None]
    stacked = jnp.stack([real_part, imag_part], axis=2).astype(jnp.bfloat16)
    return stacked.reshape(ref_wide.shape[0] * SHIFTS, 2 * ref_wide.shape[2])


def rotate_back(products, phase_cos, phase_sin):
    real_sum = jnp.sum(products[:, :, 0] * phase_cos[None] - products[:, :, 1] * phase_sin[None], axis=1)
    imag_sum = jnp.sum(products[:, :, 0] * phase_sin[None] + products[:, :, 1] * phase_cos[None], axis=1)
    return jnp.stack([real_sum, imag_sum], axis=1)


def reference(images, references, noise_weights, log_prior, groups, prior_index, class_map):
    phase_cos, phase_sin = phase_tables(HALF)
    weight_rows = noise_weights[groups]
    weighted = (images.astype(jnp.float32) * weight_rows[:, None, :]).astype(jnp.bfloat16)
    image_flat = weighted.reshape(PARTICLES, 2 * HALF)
    prior_rows = log_prior[prior_index]
    ref_blocks = references.reshape(N_ORIENT, ORI_DEV, 2, HALF)
    class_blocks = class_map.reshape(N_ORIENT, ORI_DEV)

    def block_scores(block_args):
        ref_block, class_block = block_args
        ref_wide = ref_block.astype(jnp.float32)
        ref_power = ref_wide[:, 0] ** 2 + ref_wide[:, 1] ** 2
        quadratic = jnp.dot(noise_weights, ref_power.T, precision=lax.Precision.HIGHEST, preferred_element_type=jnp.float32)
        shifted = shift_references(ref_wide, phase_cos, phase_sin)
        correlation = jnp.dot(image_flat, shifted.T, preferred_element_type=jnp.float32)
        offsets = prior_rows[:, class_block] - 0.5 * quadratic[groups]
        return correlation.reshape(PARTICLES, ORI_DEV, SHIFTS) + offsets[:, :, None]

    scores = lax.map(block_scores, (ref_blocks, class_blocks))
    score_peak = jnp.max(scores, axis=(0, 2, 3))
    log_likelihood = score_peak + jnp.log(jnp.sum(jnp.exp(scores - score_peak[None, :, None, None]), axis=(0, 2, 3)))

    def block_update(score_block):
        posterior = jnp.exp(score_block - log_likelihood[:, None, None]).astype(jnp.bfloat16)
        products = jnp.dot(posterior.reshape(PARTICLES, ORI_DEV * SHIFTS).T, image_flat, preferred_element_type=jnp.float32)
        image_sums = rotate_back(products.reshape(ORI_DEV, SHIFTS, 2, HALF), phase_cos, phase_sin)
        orient_mass = jnp.sum(posterior.astype(jnp.float32), axis=2)
        noise_mass = jnp.dot(orient_mass.T, weight_rows, precision=lax.Precision.HIGHEST, preferred_element_type=jnp.float32)
        return image_sums / (noise_mass + ridge)[:, None, :]

    updated = lax.map(block_update, scores)
    return updated.reshape(ORIENTS, 2, HALF), log_likelihood
```

```python
import jax
import jax.numpy as jnp
from jax import lax
from jax.sharding import Mesh
from jax.sharding import PartitionSpec as P

BOX = 64
SHIFTS = 9


ridge = 0.01


def phase_tables(coeffs):
    coef_index = jnp.arange(coeffs, dtype=jnp.int32)
    row_id = coef_index // (BOX // 2)
    freq_y = (row_id + BOX // 2) % BOX - BOX // 2
    freq_x = coef_index % (BOX // 2)
    shift_id = jnp.arange(SHIFTS, dtype=jnp.int32)
    move_x = shift_id % 3 - 1
    move_y = shift_id // 3 - 1
    phase_angle = (move_x[:, None] * freq_x[None, :] + move_y[:, None] * freq_y[None, :]).astype(
        jnp.float32
    ) * (2.0 * jnp.pi / BOX)
    return (jnp.cos(phase_angle), jnp.sin(phase_angle))


def shift_references(ref_wide, phase_cos, phase_sin):
    real_part = (
        ref_wide[:, None, 0, :] * phase_cos[None] + ref_wide[:, None, 1, :] * phase_sin[None]
    )
    imag_part = (
        ref_wide[:, None, 1, :] * phase_cos[None] - ref_wide[:, None, 0, :] * phase_sin[None]
    )
    stacked = jnp.stack([real_part, imag_part], axis=2).astype(jnp.bfloat16)
    return stacked.reshape(ref_wide.shape[0] * SHIFTS, 2 * ref_wide.shape[2])


def rotate_back(products, phase_cos, phase_sin):
    real_sum = jnp.sum(
        products[:, :, 0] * phase_cos[None] - products[:, :, 1] * phase_sin[None], axis=1
    )
    imag_sum = jnp.sum(
        products[:, :, 0] * phase_sin[None] + products[:, :, 1] * phase_cos[None], axis=1
    )
    return jnp.stack([real_sum, imag_sum], axis=1)


def exchange(row, axes, count):
    spread = jnp.broadcast_to(row[None, None, :], (count, 1, row.shape[0]))
    return lax.all_to_all(spread, axes, 0, 0, tiled=True)[:, 0, :]


def log_sum(rows):
    peak = jnp.max(rows, axis=0)
    return peak + jnp.log(jnp.sum(jnp.exp(rows - peak[None]), axis=0))


def shards(images, references, noise_weights, log_prior, groups, prior_index, class_map):
    particle_rows = images.shape[0]
    orient_rows = references.shape[0]
    coeffs = images.shape[2]
    highest = lax.Precision.HIGHEST
    phase_cos, phase_sin = phase_tables(coeffs)
    group_hot = (
        groups[:, None] == jnp.arange(noise_weights.shape[0], dtype=jnp.int32)[None, :]
    ).astype(jnp.float32)
    weight_rows = jnp.dot(
        group_hot, noise_weights, precision=highest, preferred_element_type=jnp.float32
    )
    weighted = (images.astype(jnp.float32) * weight_rows[:, None, :]).astype(jnp.bfloat16)
    image_flat = weighted.reshape(particle_rows, 2 * coeffs)
    ref_wide = references.astype(jnp.float32)
    ref_power = ref_wide[:, 0] ** 2 + ref_wide[:, 1] ** 2
    quadratic = jnp.dot(
        noise_weights, ref_power.T, precision=highest, preferred_element_type=jnp.float32
    )
    shifted = shift_references(ref_wide, phase_cos, phase_sin)
    correlation = lax.dot_general(
        image_flat, shifted, (((1,), (1,)), ((), ())), preferred_element_type=jnp.float32
    )
    prior_hot = (
        prior_index[:, None] == jnp.arange(log_prior.shape[0], dtype=jnp.int32)[None, :]
    ).astype(jnp.float32)
    class_hot = (
        class_map[:, None] == jnp.arange(log_prior.shape[1], dtype=jnp.int32)[None, :]
    ).astype(jnp.float32)
    prior_table = jnp.dot(
        prior_hot, log_prior, precision=highest, preferred_element_type=jnp.float32
    )
    prior_rows = jnp.dot(
        prior_table, class_hot.T, precision=highest, preferred_element_type=jnp.float32
    )
    quad_rows = jnp.dot(group_hot, quadratic, precision=highest, preferred_element_type=jnp.float32)
    scores = (
        correlation.reshape(particle_rows, orient_rows, SHIFTS)
        + (prior_rows - 0.5 * quad_rows)[:, :, None]
    )
    local_peak = jnp.max(scores, axis=(1, 2))
    local_mass = jnp.sum(jnp.exp(scores - local_peak[:, None, None]), axis=(1, 2))
    partial = local_peak + jnp.log(local_mass)
    partial = log_sum(exchange(partial, "z", 16))
    log_likelihood = log_sum(exchange(partial, ("x", "core"), 8))
    posterior = jnp.exp(scores - log_likelihood[:, None, None]).astype(jnp.bfloat16)
    products = lax.dot_general(
        posterior.reshape(particle_rows, orient_rows * SHIFTS),
        image_flat,
        (((0,), (0,)), ((), ())),
        preferred_element_type=jnp.float32,
    )
    image_sums = rotate_back(products.reshape(orient_rows, SHIFTS, 2, coeffs), phase_cos, phase_sin)
    orient_mass = jnp.sum(posterior.astype(jnp.float32), axis=2)
    group_mass = lax.dot_general(
        orient_mass,
        group_hot,
        (((0,), (0,)), ((), ())),
        precision=highest,
        preferred_element_type=jnp.float32,
    )
    parts = 4
    width = coeffs // parts
    blocks = image_sums.reshape(2 * orient_rows, parts, width).transpose(1, 0, 2)
    mass_rows = jnp.pad(group_mass.reshape(-1), (0, 8 * width - group_mass.size)).reshape(8, width)
    blocks = jnp.concatenate(
        [blocks, jnp.broadcast_to(mass_rows[None], (parts, 8, width))], axis=1
    )
    received = jnp.sum(lax.all_to_all(blocks, "dom", 0, 0, tiled=True), axis=0)
    summed_images = received[: 2 * orient_rows].reshape(orient_rows, 2, width)
    summed_mass = received[2 * orient_rows :].reshape(-1)[: group_mass.size]
    my_weights = lax.dynamic_slice_in_dim(
        noise_weights, lax.axis_index("dom") * width, width, axis=1
    )
    mass_share = jnp.dot(
        summed_mass.reshape(group_mass.shape),
        my_weights,
        precision=highest,
        preferred_element_type=jnp.float32,
    )
    new_references = summed_images / (mass_share + ridge)[:, None, :]
    return (new_references, log_likelihood)


def solution(mesh):
    fine = Mesh(mesh.devices.reshape(16, 4, 2, 4), ("z", "x", "core", "dom"))
    orient = ("z", "x", "core")
    in_specs = (
        P("dom", None, None),
        P(orient, None, None),
        P(),
        P(),
        P("dom"),
        P("dom"),
        P(orient),
    )
    out_specs = (P(orient, None, "dom"), P("dom"))
    return jax.shard_map(shards, mesh=fine, in_specs=in_specs, out_specs=out_specs, check_vma=False)
```

```python
import functools

import jax
import jax.numpy as jnp
import numpy as np
from jax import lax
from jax.experimental import pallas as pl
from jax.experimental.pallas import tpu as pltpu
from jax.sharding import Mesh
from jax.sharding import PartitionSpec as P

BOX = 64
RIDGE = 0.01
LANES = 128
PAIRS = (5, 6, 7, 8)
LOWEST = -1.0e30
HIGHEST = lax.Precision.HIGHEST
VMEM_BYTES = 50 * 1024 * 1024


def phase_tables(coeffs):
    index = np.arange(coeffs)
    row = index // (BOX // 2)
    freq_y = (row + BOX // 2) % BOX - BOX // 2
    freq_x = index % (BOX // 2)
    shift = np.array(PAIRS)
    turns = (shift % 3 - 1)[:, None] * freq_x[None] + (shift // 3 - 1)[:, None] * freq_y[None]
    angle = (turns % BOX) * (2.0 * np.pi / BOX)
    return np.concatenate([np.cos(angle), np.sin(angle)]).astype(np.float32)


def split_bf16(values):
    high = values.astype(jnp.bfloat16)
    rest = values - high.astype(jnp.float32)
    mid = rest.astype(jnp.bfloat16)
    low = (rest - mid.astype(jnp.float32)).astype(jnp.bfloat16)
    return high, mid, low


def log_sum(rows):
    peak = jnp.max(rows, axis=0, keepdims=True)
    return peak + jnp.log(jnp.sum(jnp.exp(rows - peak), axis=0, keepdims=True))


def hot_columns(count, index_row):
    rows = lax.broadcasted_iota(jnp.int32, (count, index_row.shape[1]), 0)
    return rows == index_row


def score_kernel(
    images_ref,
    refs_ref,
    noise_ref,
    prior_ref,
    groups_ref,
    prior_index_ref,
    class_ref,
    phase_ref,
    scores_ref,
    weighted_ref,
    partial_ref,
    images_vmem,
    image_wide,
    ref_wide,
    shifted,
    weights,
    power,
    image_sem,
):
    particles = groups_ref.shape[1]
    coeffs = noise_ref.shape[1]
    ngroups = noise_ref.shape[0]
    blocks = coeffs // LANES
    orients = class_ref.shape[0]
    padded = (orients + 7) // 8 * 8
    stride = 2 * blocks
    fetch = pltpu.make_async_copy(images_ref, images_vmem, image_sem)
    fetch.start()

    ref_wide[0 : orients * stride, :] = refs_ref[...].astype(jnp.float32)
    ref_wide[orients * stride :, :] = jnp.zeros(
        ((padded - orients) * stride, LANES), jnp.float32
    )
    group_hot = hot_columns(ngroups, groups_ref[...])
    group_bf16 = group_hot.astype(jnp.float32).astype(jnp.bfloat16)
    noise_parts = jnp.concatenate(split_bf16(noise_ref[...]), axis=0)
    weights[...] = lax.dot_general(
        jnp.concatenate([group_bf16] * 3, axis=0),
        noise_parts,
        (((0,), (0,)), ((), ())),
        preferred_element_type=jnp.float32,
    )

    @pl.loop(0, blocks)
    def _(b):
        here = pl.ds(pl.multiple_of(b * LANES, LANES), LANES)
        real = ref_wide[pl.ds(2 * b, padded, stride=stride), :]
        imag = ref_wide[pl.ds(2 * b + 1, padded, stride=stride), :]
        power[:, here] = real * real + imag * imag
        reals = [real, jnp.zeros((8, LANES), jnp.float32)]
        imags = [imag, jnp.zeros((8, LANES), jnp.float32)]
        for k in range(4):
            cosine = phase_ref[k : k + 1, here]
            sine = phase_ref[k + 4 : k + 5, here]
            real_cos, real_sin = real * cosine, real * sine
            imag_cos, imag_sin = imag * cosine, imag * sine
            reals += [real_cos + imag_sin, real_cos - imag_sin]
            imags += [imag_cos - real_sin, imag_cos + real_sin]
        wide = pl.multiple_of(b * 2 * LANES, 2 * LANES)
        shifted[:, pl.ds(wide, LANES)] = jnp.concatenate(reals, axis=0).astype(jnp.bfloat16)
        shifted[:, pl.ds(wide + LANES, LANES)] = jnp.concatenate(imags, axis=0).astype(
            jnp.bfloat16
        )

    quadratic = lax.dot_general(
        power[...],
        noise_ref[...],
        (((1,), (1,)), ((), ())),
        precision=HIGHEST,
        preferred_element_type=jnp.float32,
    )
    classes = prior_ref.shape[1]
    class_hot = (
        lax.broadcasted_iota(jnp.int32, (orients, classes), 1) == class_ref[...]
    ).astype(jnp.float32)
    class_hot = jnp.concatenate(
        [class_hot, jnp.zeros((padded - orients, classes), jnp.float32)], axis=0
    )
    class_prior = lax.dot_general(
        class_hot,
        prior_ref[...],
        (((1,), (1,)), ((), ())),
        precision=HIGHEST,
        preferred_element_type=jnp.float32,
    )
    prior_hot = hot_columns(prior_ref.shape[0], prior_index_ref[...]).astype(jnp.float32)
    offsets = jnp.dot(
        class_prior, prior_hot, precision=HIGHEST, preferred_element_type=jnp.float32
    ) - 0.5 * jnp.dot(
        quadratic,
        group_hot.astype(jnp.float32),
        precision=HIGHEST,
        preferred_element_type=jnp.float32,
    )
    real_row = lax.broadcasted_iota(jnp.int32, (padded, particles), 0) < orients
    offsets = jnp.where(real_row, offsets, LOWEST)

    fetch.wait()

    @pl.loop(0, blocks)
    def _(b):
        part = particles // blocks * stride
        rows = pl.ds(pl.multiple_of(b * part, part), part)
        image_wide[rows, :] = images_vmem[rows, :].astype(jnp.float32)

    @pl.loop(0, blocks)
    def _(b):
        here = pl.ds(pl.multiple_of(b * LANES, LANES), LANES)
        weight = weights[:, here]
        wide = pl.multiple_of(b * 2 * LANES, 2 * LANES)
        for part in range(2):
            picked = image_wide[pl.ds(2 * b + part, particles, stride=stride), :]
            weighted_ref[:, pl.ds(wide + part * LANES, LANES)] = (picked * weight).astype(
                jnp.bfloat16
            )

    correlation = lax.dot_general(
        shifted[...],
        weighted_ref[...],
        (((1,), (1,)), ((), ())),
        preferred_element_type=jnp.float32,
    )
    scores = correlation + jnp.concatenate(
        [offsets, jnp.full((8, particles), LOWEST, jnp.float32)] + [offsets] * 8, axis=0
    )
    scores_ref[...] = scores
    partial_ref[...] = jnp.broadcast_to(log_sum(scores)[None], partial_ref.shape)


def update_kernel(
    partial_ref, scores_ref, weighted_ref, groups_ref, phase_ref, ngroups, likelihood_ref, out_ref
):
    orients = (out_ref.shape[1] - 8) // 2
    padded = (orients + 7) // 8 * 8
    width = out_ref.shape[2]
    likelihood = log_sum(partial_ref[:, 0, :])
    likelihood_ref[...] = likelihood
    posterior = jnp.exp(scores_ref[...] - likelihood).astype(jnp.bfloat16)
    group_hot = hot_columns(ngroups, groups_ref[...]).astype(jnp.float32).astype(jnp.bfloat16)
    mass = lax.dot_general(
        posterior, group_hot, (((1,), (1,)), ((), ())), preferred_element_type=jnp.float32
    )
    group_mass = mass[0:padded]
    for k in range(8):
        group_mass += mass[48 + k * padded : 48 + (k + 1) * padded]
    pieces = [group_mass[r : r + 8] for r in range(0, padded, 8)]
    room = width - ngroups * len(pieces)
    mass_rows = jnp.concatenate(pieces + [jnp.zeros((8, room), jnp.float32)], axis=1)
    for share in range(out_ref.shape[0]):
        out_ref[share, 2 * orients :, :] = mass_rows
        for step in range(width // LANES):
            b = share * (width // LANES) + step
            here = slice(b * LANES, (b + 1) * LANES)
            product = jnp.dot(
                posterior,
                weighted_ref[:, 2 * b * LANES : 2 * (b + 1) * LANES],
                preferred_element_type=jnp.float32,
            )
            real = product[0:padded, 0:LANES]
            imag = product[0:padded, LANES:]
            for k in range(4):
                cosine = phase_ref[k : k + 1, here]
                sine = phase_ref[k + 4 : k + 5, here]
                low = 48 + 2 * padded * k
                ahead = product[low : low + padded]
                behind = product[low + padded : low + 2 * padded]
                both, apart = ahead + behind, ahead - behind
                real += both[:, 0:LANES] * cosine - apart[:, LANES:] * sine
                imag += apart[:, 0:LANES] * sine + both[:, LANES:] * cosine
            there = slice(step * LANES, (step + 1) * LANES)
            out_ref[share, 0:orients, there] = real[0:orients]
            out_ref[share, orients : 2 * orients, there] = imag[0:orients]


def divide_kernel(share_ref, received_ref, noise_ref, out_ref):
    del share_ref
    rows = received_ref.shape[1]
    width = received_ref.shape[2]
    orients = (rows - 8) // 2
    padded = (orients + 7) // 8 * 8
    ngroups = noise_ref.shape[0]
    total = received_ref[0]
    for peer in range(1, received_ref.shape[0]):
        total += received_ref[peer]
    packed = total[2 * orients :]
    group_mass = jnp.concatenate(
        [packed[:, r * ngroups : (r + 1) * ngroups] for r in range(padded // 8)], axis=0
    )
    noise_mass = jnp.dot(
        group_mass, noise_ref[...], precision=HIGHEST, preferred_element_type=jnp.float32
    )
    scale = 1.0 / (noise_mass[0:orients] + RIDGE)
    for part in range(2):
        values = total[part * orients : (part + 1) * orients] * scale
        for b in range(width // LANES):
            out_ref[pl.ds(2 * b + part, orients, stride=2 * (width // LANES)), :] = values[
                :, b * LANES : (b + 1) * LANES
            ]


def rows_of(array):
    count, parts, coeffs = array.shape
    blocks = coeffs // LANES
    return (
        array.reshape(count, parts, blocks, LANES)
        .transpose(0, 2, 1, 3)
        .reshape(count * blocks * parts, LANES)
    )


def kernel_params():
    return pltpu.CompilerParams(vmem_limit_bytes=VMEM_BYTES)


def score_call(images, references, noise_weights, log_prior, groups, prior_index, class_map, phase, spread):
    particles, _, coeffs = images.shape
    orients = references.shape[0]
    padded = (orients + 7) // 8 * 8
    rows = 9 * padded + 8
    whole = pl.BlockSpec(memory_space=pltpu.VMEM)
    return pl.pallas_call(
        score_kernel,
        in_specs=[pl.BlockSpec(memory_space=pl.ANY)] + [whole] * 7,
        out_specs=[whole] * 3,
        out_shape=[
            jax.ShapeDtypeStruct((rows, particles), jnp.float32),
            jax.ShapeDtypeStruct((particles, 2 * coeffs), jnp.bfloat16),
            jax.ShapeDtypeStruct((spread, 1, particles), jnp.float32),
        ],
        scratch_shapes=[
            pltpu.VMEM((particles * 2 * coeffs // LANES, LANES), jnp.bfloat16),
            pltpu.VMEM((particles * 2 * coeffs // LANES, LANES), jnp.float32),
            pltpu.VMEM((padded * 2 * coeffs // LANES, LANES), jnp.float32),
            pltpu.VMEM((rows, 2 * coeffs), jnp.bfloat16),
            pltpu.VMEM((particles, coeffs), jnp.float32),
            pltpu.VMEM((padded, coeffs), jnp.float32),
            pltpu.SemaphoreType.DMA,
        ],
        compiler_params=kernel_params(),
        name="score",
    )(
        rows_of(images),
        rows_of(references),
        noise_weights,
        log_prior,
        groups[None, :],
        prior_index[None, :],
        class_map[:, None],
        phase,
    )


def update_call(partials, scores, weighted, groups, phase, ngroups, orients, shares):
    particles, wide = weighted.shape
    whole = pl.BlockSpec(memory_space=pltpu.VMEM)

    def body(partial_ref, scores_ref, weighted_ref, groups_ref, phase_ref, likelihood_ref, out_ref):
        update_kernel(
            partial_ref, scores_ref, weighted_ref, groups_ref, phase_ref, ngroups, likelihood_ref, out_ref
        )

    return pl.pallas_call(
        body,
        in_specs=[whole] * 5,
        out_specs=[whole] * 2,
        out_shape=[
            jax.ShapeDtypeStruct((1, particles), jnp.float32),
            jax.ShapeDtypeStruct((shares, 2 * orients + 8, wide // 2 // shares), jnp.float32),
        ],
        compiler_params=kernel_params(),
        name="update",
    )(partials, scores, weighted, groups[None, :], phase)


def divide_call(share, received, noise_weights):
    shares, rows, width = received.shape
    orients = (rows - 8) // 2
    ngroups = noise_weights.shape[0]
    return pl.pallas_call(
        divide_kernel,
        grid_spec=pltpu.PrefetchScalarGridSpec(
            num_scalar_prefetch=1,
            grid=(1,),
            in_specs=[
                pl.BlockSpec((shares, rows, width), lambda i, s: (0, 0, 0)),
                pl.BlockSpec((ngroups, width), lambda i, s: (0, s[0])),
            ],
            out_specs=pl.BlockSpec((orients * 2 * width // LANES, LANES), lambda i, s: (0, 0)),
        ),
        out_shape=jax.ShapeDtypeStruct((orients * 2 * width // LANES, LANES), jnp.float32),
        compiler_params=kernel_params(),
        name="divide",
    )(share, received, noise_weights)


def exchange(spread, axes):
    return lax.all_to_all(spread, axes, 0, 0, tiled=True)


def shards(images, references, noise_weights, log_prior, groups, prior_index, class_map):
    coeffs = images.shape[2]
    orients = references.shape[0]
    phase = jnp.asarray(phase_tables(coeffs))
    depth = lax.axis_size("z")
    plane = lax.axis_size("x") * lax.axis_size("core")
    shares = lax.axis_size("dom")
    scores, weighted, partial = score_call(
        images, references, noise_weights, log_prior, groups, prior_index, class_map, phase, depth
    )
    partial = log_sum(exchange(partial, "z")[:, 0, :])
    partial = jnp.broadcast_to(partial[None], (plane, 1, partial.shape[1]))
    partials = exchange(partial, ("x", "core"))
    likelihood, blocks = update_call(
        partials, scores, weighted, groups, phase, noise_weights.shape[0], orients, shares
    )
    received = exchange(blocks, "dom")
    share = lax.axis_index("dom").astype(jnp.int32)[None]
    new_rows = divide_call(share, received, noise_weights)
    width = coeffs // shares
    new_references = (
        new_rows.reshape(orients, width // LANES, 2, LANES)
        .transpose(0, 2, 1, 3)
        .reshape(orients, 2, width)
    )
    return (new_references, likelihood[0])


def solution(mesh):
    fine = Mesh(mesh.devices.reshape(16, 4, 2, 4), ("z", "x", "core", "dom"))
    orient = ("z", "x", "core")
    in_specs = (
        P("dom", None, None),
        P(orient, None, None),
        P(),
        P(),
        P("dom"),
        P("dom"),
        P(orient),
    )
    out_specs = (P(orient, None, "dom"), P("dom"))
    return jax.shard_map(shards, mesh=fine, in_specs=in_specs, out_specs=out_specs, check_vma=False)
```

```python
import functools

import jax
import jax.numpy as jnp
import numpy as np
from jax import lax
from jax.experimental import pallas as pl
from jax.experimental.pallas import tpu as pltpu
from jax.sharding import Mesh
from jax.sharding import PartitionSpec as P

BOX = 64
RIDGE = 0.01
LANES = 128
PAIRS = (5, 6, 7, 8)
LOWEST = -1.0e30
HIGHEST = lax.Precision.HIGHEST
SCORE_VMEM = 36 * 1024 * 1024
OTHER_VMEM = 24 * 1024 * 1024


def phase_tables(coeffs):
    index = np.arange(coeffs)
    row = index // (BOX // 2)
    freq_y = (row + BOX // 2) % BOX - BOX // 2
    freq_x = index % (BOX // 2)
    shift = np.array(PAIRS)
    turns = (shift % 3 - 1)[:, None] * freq_x[None] + (shift // 3 - 1)[:, None] * freq_y[None]
    angle = (turns % BOX) * (2.0 * np.pi / BOX)
    return np.concatenate([np.cos(angle), np.sin(angle)]).astype(np.float32)


def split_bf16(values):
    high = values.astype(jnp.bfloat16)
    rest = values - high.astype(jnp.float32)
    mid = rest.astype(jnp.bfloat16)
    low = (rest - mid.astype(jnp.float32)).astype(jnp.bfloat16)
    return high, mid, low


def log_sum(rows):
    peak = jnp.max(rows, axis=0, keepdims=True)
    return peak + jnp.log(jnp.sum(jnp.exp(rows - peak), axis=0, keepdims=True))


def hot_columns(count, index_row):
    rows = lax.broadcasted_iota(jnp.int32, (count, index_row.shape[1]), 0)
    return rows == index_row


def score_kernel(
    images_hbm,
    refs_hbm,
    noise_hbm,
    prior_hbm,
    groups_hbm,
    prior_index_hbm,
    class_hbm,
    phase_hbm,
    scores_ref,
    weighted_ref,
    partial_ref,
    images_ref,
    refs_ref,
    noise_ref,
    prior_ref,
    groups_ref,
    prior_index_ref,
    class_ref,
    phase_ref,
    image_wide,
    ref_wide,
    shifted,
    weights,
    power,
    sems,
):
    particles = groups_ref.shape[0]
    coeffs = noise_ref.shape[1]
    ngroups = noise_ref.shape[0]
    blocks = coeffs // LANES
    orients = class_ref.shape[0]
    padded = (orients + 7) // 8 * 8
    rows = 2 * blocks
    pitch = rows + 1
    pairs = (
        (refs_hbm, refs_ref),
        (phase_hbm, phase_ref),
        (groups_hbm, groups_ref),
        (noise_hbm, noise_ref),
        (prior_index_hbm, prior_index_ref),
        (class_hbm, class_ref),
        (prior_hbm, prior_ref),
        (images_hbm, images_ref),
    )
    fetches = [pltpu.make_async_copy(*pair, sems.at[i]) for i, pair in enumerate(pairs)]
    for fetch in fetches:
        fetch.start()
    for fetch in fetches[:3]:
        fetch.wait()
    tables = 9 * padded + 8 + ngroups
    for b in range(blocks):
        scores_ref[tables + 8 * b : tables + 8 * b + 8, 0:LANES] = phase_ref[
            :, b * LANES : (b + 1) * LANES
        ]

    def spread(source, target, first, count):
        for k in range(count):
            wide = source[pl.ds((first + k) * rows, rows), :].astype(jnp.float32)
            for step in range(0, rows, 8):
                target[pl.ds(pl.multiple_of(first * pitch, 8) + k * pitch + step, 8), :] = wide[
                    step : step + 8
                ]

    for first in range(0, orients, 8):
        spread(refs_ref, ref_wide, first, min(8, orients - first))
    ref_wide[orients * pitch :, :] = jnp.zeros(
        (ref_wide.shape[0] - orients * pitch, LANES), jnp.float32
    )
    group_hot = hot_columns(ngroups, groups_ref[...].reshape(1, particles))
    group_hot = group_hot.astype(jnp.float32)
    scores_ref[9 * padded + 8 : tables] = group_hot
    group_hot = group_hot.astype(jnp.bfloat16)
    @pl.loop(0, blocks)
    def _(b):
        here = pl.ds(pl.multiple_of(b * LANES, LANES), LANES)
        real = ref_wide[pl.ds(2 * b, padded, stride=pitch), :]
        imag = ref_wide[pl.ds(2 * b + 1, padded, stride=pitch), :]
        power[:, here] = jnp.concatenate(split_bf16(real * real + imag * imag), axis=0)
        reals = [real, jnp.zeros((8, LANES), jnp.float32)]
        imags = [imag, jnp.zeros((8, LANES), jnp.float32)]
        for k in range(4):
            cosine = phase_ref[k : k + 1, here]
            sine = phase_ref[k + 4 : k + 5, here]
            real_cos, real_sin = real * cosine, real * sine
            imag_cos, imag_sin = imag * cosine, imag * sine
            reals += [real_cos + imag_sin, real_cos - imag_sin]
            imags += [imag_cos - real_sin, imag_cos + real_sin]
        wide = pl.multiple_of(b * 2 * LANES, 2 * LANES)
        shifted[:, pl.ds(wide, LANES)] = jnp.concatenate(reals, axis=0).astype(jnp.bfloat16)
        shifted[:, pl.ds(wide + LANES, LANES)] = jnp.concatenate(imags, axis=0).astype(
            jnp.bfloat16
        )

    fetches[3].wait()
    noise_parts = jnp.concatenate(split_bf16(noise_ref[...]), axis=0)
    weights[...] = lax.dot_general(
        jnp.concatenate([group_hot] * 3, axis=0),
        noise_parts,
        (((0,), (0,)), ((), ())),
        preferred_element_type=jnp.float32,
    )
    products = lax.dot_general(
        power[...], noise_parts, (((1,), (1,)), ((), ())), preferred_element_type=jnp.float32
    )
    products = products[0:padded] + products[padded : 2 * padded] + products[2 * padded :]
    quadratic = (
        products[:, 0:ngroups]
        + products[:, ngroups : 2 * ngroups]
        + products[:, 2 * ngroups : 3 * ngroups]
    )
    for fetch in fetches[4:7]:
        fetch.wait()
    class_hot = hot_columns(prior_ref.shape[1], class_ref[...].reshape(1, orients))
    class_prior = lax.dot_general(
        class_hot.astype(jnp.float32),
        prior_ref[...],
        (((0,), (1,)), ((), ())),
        precision=HIGHEST,
        preferred_element_type=jnp.float32,
    )
    class_prior = jnp.concatenate(
        [class_prior, jnp.zeros((padded - orients, prior_ref.shape[0]), jnp.float32)], axis=0
    )
    prior_hot = hot_columns(prior_ref.shape[0], prior_index_ref[...].reshape(1, particles))
    prior_hot = prior_hot.astype(jnp.float32)
    offsets = jnp.dot(
        jnp.concatenate(split_bf16(-0.5 * quadratic), axis=1),
        jnp.concatenate([group_hot] * 3, axis=0),
        preferred_element_type=jnp.float32,
    ) + jnp.dot(class_prior, prior_hot, precision=HIGHEST, preferred_element_type=jnp.float32)
    real_row = lax.broadcasted_iota(jnp.int32, (padded, particles), 0) < orients
    offsets = jnp.where(real_row, offsets, LOWEST)

    fetches[7].wait()

    @pl.loop(0, particles // 8)
    def _(g):
        spread(images_ref, image_wide, g * 8, 8)

    @pl.loop(0, blocks)
    def _(b):
        here = pl.ds(pl.multiple_of(b * LANES, LANES), LANES)
        weight = weights[:, here]
        wide = pl.multiple_of(b * 2 * LANES, 2 * LANES)
        for part in range(2):
            picked = image_wide[pl.ds(2 * b + part, particles, stride=pitch), :]
            weighted_ref[:, pl.ds(wide + part * LANES, LANES)] = (picked * weight).astype(
                jnp.bfloat16
            )

    correlation = lax.dot_general(
        shifted[...],
        weighted_ref[...],
        (((1,), (1,)), ((), ())),
        preferred_element_type=jnp.float32,
    )
    scores = correlation + jnp.concatenate(
        [offsets, jnp.full((8, particles), LOWEST, jnp.float32)] + [offsets] * 8, axis=0
    )
    scores_ref[0 : 9 * padded + 8] = scores
    partial_ref[...] = jnp.broadcast_to(log_sum(scores)[None], partial_ref.shape)


def update_kernel(
    ngroups, partial_ref, scores_ref, weighted_ref, likelihood_ref, out_hbm, out_ref, sems
):
    orients = (out_ref.shape[1] - 8) // 2
    padded = (orients + 7) // 8 * 8
    width = out_ref.shape[2]
    stores = [
        pltpu.make_async_copy(out_ref.at[share], out_hbm.at[share], sems.at[share])
        for share in range(out_ref.shape[0])
    ]
    likelihood = log_sum(partial_ref[:, 0, :])
    likelihood_ref[...] = likelihood
    rows = 9 * padded + 8
    posterior = jnp.exp(scores_ref[0:rows] - likelihood).astype(jnp.bfloat16)
    group_hot = scores_ref[rows : rows + ngroups].astype(jnp.bfloat16)
    mass = lax.dot_general(
        posterior, group_hot, (((1,), (1,)), ((), ())), preferred_element_type=jnp.float32
    )
    group_mass = mass[0:padded]
    for k in range(8):
        group_mass += mass[48 + k * padded : 48 + (k + 1) * padded]
    pieces = [group_mass[r : r + 8] for r in range(0, padded, 8)]
    room = width - ngroups * len(pieces)
    mass_rows = jnp.concatenate(pieces + [jnp.zeros((8, room), jnp.float32)], axis=1)
    for share in range(out_ref.shape[0]):
        out_ref[share, 2 * orients :, :] = mass_rows
        for step in range(width // LANES):
            b = share * (width // LANES) + step
            table = rows + ngroups + 8 * b
            product = jnp.dot(
                posterior,
                weighted_ref[:, 2 * b * LANES : 2 * (b + 1) * LANES],
                preferred_element_type=jnp.float32,
            )
            real = product[0:padded, 0:LANES]
            imag = product[0:padded, LANES:]
            for k in range(4):
                cosine = scores_ref[table + k : table + k + 1, 0:LANES]
                sine = scores_ref[table + k + 4 : table + k + 5, 0:LANES]
                low = 48 + 2 * padded * k
                ahead = product[low : low + padded]
                behind = product[low + padded : low + 2 * padded]
                both, apart = ahead + behind, ahead - behind
                real += both[:, 0:LANES] * cosine - apart[:, LANES:] * sine
                imag += apart[:, 0:LANES] * sine + both[:, LANES:] * cosine
            there = slice(step * LANES, (step + 1) * LANES)
            out_ref[share, 0:orients, there] = real[0:orients]
            out_ref[share, orients : 2 * orients, there] = imag[0:orients]
        stores[share].start()
    for store in stores:
        store.wait()


def divide_kernel(share_ref, received_ref, noise_ref, out_ref):
    del share_ref
    rows = received_ref.shape[1]
    width = received_ref.shape[2]
    orients = (rows - 8) // 2
    padded = (orients + 7) // 8 * 8
    ngroups = noise_ref.shape[0]
    total = received_ref[0]
    for peer in range(1, received_ref.shape[0]):
        total += received_ref[peer]
    packed = total[2 * orients :]
    group_mass = jnp.concatenate(
        [packed[:, r * ngroups : (r + 1) * ngroups] for r in range(padded // 8)], axis=0
    )
    noise_mass = jnp.dot(
        group_mass, noise_ref[...], precision=HIGHEST, preferred_element_type=jnp.float32
    )
    scale = 1.0 / (noise_mass[0:orients] + RIDGE)
    for part in range(2):
        values = total[part * orients : (part + 1) * orients] * scale
        for b in range(width // LANES):
            out_ref[pl.ds(2 * b + part, orients, stride=2 * (width // LANES)), :] = values[
                :, b * LANES : (b + 1) * LANES
            ]


def rows_of(array):
    count, parts, coeffs = array.shape
    blocks = coeffs // LANES
    return (
        array.reshape(count, parts, blocks, LANES)
        .transpose(0, 2, 1, 3)
        .reshape(count * blocks * parts, LANES)
    )


def kernel_params(limit):
    return pltpu.CompilerParams(vmem_limit_bytes=limit)


def score_call(images, references, noise_weights, log_prior, groups, prior_index, class_map, phase, spread):
    particles, _, coeffs = images.shape
    orients = references.shape[0]
    padded = (orients + 7) // 8 * 8
    rows = 9 * padded + 8
    ngroups = noise_weights.shape[0]
    operands = [
        rows_of(images),
        rows_of(references),
        noise_weights,
        log_prior,
        groups,
        prior_index,
        class_map,
        phase,
    ]
    return pl.pallas_call(
        score_kernel,
        in_specs=[pl.BlockSpec(memory_space=pltpu.HBM)] * 8,
        out_specs=[pl.BlockSpec(memory_space=pltpu.VMEM)] * 3,
        out_shape=[
            pltpu.VMEM((rows + ngroups + 8 * coeffs // LANES, particles), jnp.float32),
            pltpu.VMEM((particles, 2 * coeffs), jnp.bfloat16),
            jax.ShapeDtypeStruct((spread, 1, particles), jnp.float32),
        ],
        scratch_shapes=[pltpu.VMEM(array.shape, array.dtype) for array in operands]
        + [
            pltpu.VMEM((particles * (2 * coeffs // LANES + 1), LANES), jnp.float32),
            pltpu.VMEM((padded * (2 * coeffs // LANES + 1), LANES), jnp.float32),
            pltpu.VMEM((rows, 2 * coeffs), jnp.bfloat16),
            pltpu.VMEM((particles, coeffs), jnp.float32),
            pltpu.VMEM((3 * padded, coeffs), jnp.bfloat16),
            pltpu.SemaphoreType.DMA((8,)),
        ],
        compiler_params=kernel_params(SCORE_VMEM),
        name="score",
    )(*[pltpu.with_memory_space_constraint(array, pltpu.HBM) for array in operands])


def update_call(partials, scores, weighted, ngroups, orients, shares):
    particles, wide = weighted.shape
    block = (shares, 2 * orients + 8, wide // 2 // shares)
    kept = [
        pltpu.with_memory_space_constraint(array, pltpu.VMEM)
        for array in (scores, weighted)
    ]
    whole = pl.BlockSpec(memory_space=pltpu.VMEM)

    return pl.pallas_call(
        functools.partial(update_kernel, ngroups),
        in_specs=[whole] * 3,
        out_specs=[whole, pl.BlockSpec(memory_space=pltpu.HBM)],
        out_shape=[
            jax.ShapeDtypeStruct((1, particles), jnp.float32),
            pltpu.HBM(block, jnp.float32),
        ],
        scratch_shapes=[pltpu.VMEM(block, jnp.float32), pltpu.SemaphoreType.DMA((shares,))],
        compiler_params=kernel_params(OTHER_VMEM),
        name="update",
    )(partials, *kept)


def divide_call(share, received, noise_weights):
    shares, rows, width = received.shape
    orients = (rows - 8) // 2
    ngroups = noise_weights.shape[0]
    return pl.pallas_call(
        divide_kernel,
        grid_spec=pltpu.PrefetchScalarGridSpec(
            num_scalar_prefetch=1,
            grid=(1,),
            in_specs=[
                pl.BlockSpec((shares, rows, width), lambda i, s: (0, 0, 0)),
                pl.BlockSpec((ngroups, width), lambda i, s: (0, s[0])),
            ],
            out_specs=pl.BlockSpec((orients * 2 * width // LANES, LANES), lambda i, s: (0, 0)),
        ),
        out_shape=jax.ShapeDtypeStruct((orients * 2 * width // LANES, LANES), jnp.float32),
        compiler_params=kernel_params(OTHER_VMEM),
        name="divide",
    )(
        share,
        pltpu.with_memory_space_constraint(received, pltpu.VMEM),
        pltpu.with_memory_space_constraint(noise_weights, pltpu.HBM),
    )


def exchange(spread, axes):
    return lax.all_to_all(spread, axes, 0, 0, tiled=True)


def shards(images, references, noise_weights, log_prior, groups, prior_index, class_map):
    coeffs = images.shape[2]
    orients = references.shape[0]
    phase = jnp.asarray(phase_tables(coeffs))
    depth = lax.axis_size("z")
    plane = lax.axis_size("x") * lax.axis_size("core")
    shares = lax.axis_size("dom")
    scores, weighted, partial = score_call(
        images, references, noise_weights, log_prior, groups, prior_index, class_map, phase, depth
    )
    partial = log_sum(exchange(partial, "z")[:, 0, :])
    partial = jnp.broadcast_to(partial[None], (plane, 1, partial.shape[1]))
    partials = exchange(partial, ("x", "core"))
    likelihood, blocks = update_call(
        partials, scores, weighted, noise_weights.shape[0], orients, shares
    )
    received = exchange(blocks, "dom")
    share = lax.axis_index("dom").astype(jnp.int32)[None]
    new_rows = divide_call(share, received, noise_weights)
    width = coeffs // shares
    new_references = (
        new_rows.reshape(orients, width // LANES, 2, LANES)
        .transpose(0, 2, 1, 3)
        .reshape(orients, 2, width)
    )
    return (new_references, likelihood[0])


def solution(mesh):
    fine = Mesh(mesh.devices.reshape(16, 4, 2, 4), ("z", "x", "core", "dom"))
    orient = ("z", "x", "core")
    in_specs = (
        P("dom", None, None),
        P(orient, None, None),
        P(),
        P(),
        P("dom"),
        P("dom"),
        P(orient),
    )
    out_specs = (P(orient, None, "dom"), P("dom"))
    return jax.shard_map(shards, mesh=fine, in_specs=in_specs, out_specs=out_specs, check_vma=False)
```

```python
import functools

import jax
import jax.numpy as jnp
import numpy as np
from jax import lax
from jax.experimental import pallas as pl
from jax.experimental.pallas import tpu as pltpu
from jax.sharding import Mesh
from jax.sharding import PartitionSpec as P

BOX = 64
RIDGE = 0.01
LANES = 128
PAIRS = (5, 6, 7, 8)
LOWEST = -1.0e30
HIGHEST = lax.Precision.HIGHEST
SCORE_VMEM = 36 * 1024 * 1024
OTHER_VMEM = 24 * 1024 * 1024


def phase_tables(coeffs):
    index = np.arange(coeffs)
    row = index // (BOX // 2)
    freq_y = (row + BOX // 2) % BOX - BOX // 2
    freq_x = index % (BOX // 2)
    shift = np.array(PAIRS)
    turns = (shift % 3 - 1)[:, None] * freq_x[None] + (shift // 3 - 1)[:, None] * freq_y[None]
    angle = (turns % BOX) * (2.0 * np.pi / BOX)
    return np.concatenate([np.cos(angle), np.sin(angle)]).astype(np.float32)


def split_bf16(values):
    high = values.astype(jnp.bfloat16)
    rest = values - high.astype(jnp.float32)
    mid = rest.astype(jnp.bfloat16)
    low = (rest - mid.astype(jnp.float32)).astype(jnp.bfloat16)
    return high, mid, low


def log_sum(rows):
    peak = jnp.max(rows, axis=0, keepdims=True)
    return peak + jnp.log(jnp.sum(jnp.exp(rows - peak), axis=0, keepdims=True))


def hot_columns(count, index_row):
    rows = lax.broadcasted_iota(jnp.int32, (count, index_row.shape[1]), 0)
    return rows == index_row


def score_kernel(
    images_hbm,
    refs_hbm,
    noise_hbm,
    prior_hbm,
    groups_hbm,
    prior_index_hbm,
    class_hbm,
    phase_hbm,
    scores_ref,
    weighted_ref,
    partial_ref,
    images_ref,
    refs_ref,
    noise_ref,
    prior_ref,
    groups_ref,
    prior_index_ref,
    class_ref,
    phase_ref,
    image_wide,
    ref_wide,
    shifted,
    weights,
    power,
    sems,
):
    particles = groups_ref.shape[0]
    coeffs = noise_ref.shape[1]
    ngroups = noise_ref.shape[0]
    blocks = coeffs // LANES
    orients = class_ref.shape[0]
    padded = (orients + 7) // 8 * 8
    rows = 2 * blocks
    pitch = rows + 1
    pairs = (
        (refs_hbm, refs_ref),
        (phase_hbm, phase_ref),
        (groups_hbm, groups_ref),
        (noise_hbm, noise_ref),
        (prior_index_hbm, prior_index_ref),
        (class_hbm, class_ref),
        (prior_hbm, prior_ref),
        (images_hbm, images_ref),
    )
    fetches = [pltpu.make_async_copy(*pair, sems.at[i]) for i, pair in enumerate(pairs)]
    for fetch in fetches:
        fetch.start()
    for fetch in fetches[:3]:
        fetch.wait()
    tables = 9 * padded + 8 + ngroups
    for b in range(blocks):
        scores_ref[tables + 8 * b : tables + 8 * b + 8, 0:LANES] = phase_ref[
            :, b * LANES : (b + 1) * LANES
        ]

    def spread(source, target, first, count):
        for k in range(count):
            wide = source[pl.ds((first + k) * rows, rows), :].astype(jnp.float32)
            for step in range(0, rows, 8):
                target[pl.ds(pl.multiple_of(first * pitch, 8) + k * pitch + step, 8), :] = wide[
                    step : step + 8
                ]

    for first in range(0, orients, 8):
        spread(refs_ref, ref_wide, first, min(8, orients - first))
    ref_wide[orients * pitch :, :] = jnp.zeros(
        (ref_wide.shape[0] - orients * pitch, LANES), jnp.float32
    )
    group_hot = hot_columns(ngroups, groups_ref[...].reshape(1, particles))
    group_hot = group_hot.astype(jnp.float32)
    scores_ref[9 * padded + 8 : tables] = group_hot
    group_hot = group_hot.astype(jnp.bfloat16)
    fetches[3].wait()
    noise_parts = jnp.concatenate(split_bf16(noise_ref[...]), axis=0)
    weights[...] = lax.dot_general(
        jnp.concatenate([group_hot] * 3, axis=0),
        noise_parts,
        (((0,), (0,)), ((), ())),
        preferred_element_type=jnp.float32,
    )
    for b in range(blocks):
        here = pl.ds(b * LANES, LANES)
        real = ref_wide[pl.ds(2 * b, padded, stride=pitch), :]
        imag = ref_wide[pl.ds(2 * b + 1, padded, stride=pitch), :]
        power[:, here] = jnp.concatenate(split_bf16(real * real + imag * imag), axis=0)
        reals = [real, jnp.zeros((8, LANES), jnp.float32)]
        imags = [imag, jnp.zeros((8, LANES), jnp.float32)]
        for k in range(4):
            cosine = phase_ref[k : k + 1, here]
            sine = phase_ref[k + 4 : k + 5, here]
            real_cos, real_sin = real * cosine, real * sine
            imag_cos, imag_sin = imag * cosine, imag * sine
            reals += [real_cos + imag_sin, real_cos - imag_sin]
            imags += [imag_cos - real_sin, imag_cos + real_sin]
        wide = b * 2 * LANES
        shifted[:, pl.ds(wide, LANES)] = jnp.concatenate(reals, axis=0).astype(jnp.bfloat16)
        shifted[:, pl.ds(wide + LANES, LANES)] = jnp.concatenate(imags, axis=0).astype(
            jnp.bfloat16
        )

    products = lax.dot_general(
        power[...], noise_parts, (((1,), (1,)), ((), ())), preferred_element_type=jnp.float32
    )
    products = products[0:padded] + products[padded : 2 * padded] + products[2 * padded :]
    quadratic = (
        products[:, 0:ngroups]
        + products[:, ngroups : 2 * ngroups]
        + products[:, 2 * ngroups : 3 * ngroups]
    )
    for fetch in fetches[4:7]:
        fetch.wait()
    class_hot = hot_columns(prior_ref.shape[1], class_ref[...].reshape(1, orients))
    class_prior = lax.dot_general(
        class_hot.astype(jnp.float32),
        prior_ref[...],
        (((0,), (1,)), ((), ())),
        precision=HIGHEST,
        preferred_element_type=jnp.float32,
    )
    class_prior = jnp.concatenate(
        [class_prior, jnp.zeros((padded - orients, prior_ref.shape[0]), jnp.float32)], axis=0
    )
    prior_hot = hot_columns(prior_ref.shape[0], prior_index_ref[...].reshape(1, particles))
    prior_hot = prior_hot.astype(jnp.float32)
    offsets = jnp.dot(
        jnp.concatenate(split_bf16(-0.5 * quadratic), axis=1),
        jnp.concatenate([group_hot] * 3, axis=0),
        preferred_element_type=jnp.float32,
    ) + jnp.dot(class_prior, prior_hot, precision=HIGHEST, preferred_element_type=jnp.float32)
    real_row = lax.broadcasted_iota(jnp.int32, (padded, particles), 0) < orients
    offsets = jnp.where(real_row, offsets, LOWEST)

    scores_ref[0 : 9 * padded + 8] = jnp.concatenate(
        [offsets, jnp.full((8, particles), LOWEST, jnp.float32)] + [offsets] * 8, axis=0
    )
    fetches[7].wait()

    @pl.loop(0, particles // 32)
    def _(g):
        for h in range(4):
            spread(images_ref, image_wide, g * 32 + h * 8, 8)

    total = None
    for b in range(blocks):
        weight = weights[:, pl.ds(b * LANES, LANES)]
        wide = pl.ds(b * 2 * LANES, 2 * LANES)
        both = [
            image_wide[pl.ds(2 * b + part, particles, stride=pitch), :] * weight
            for part in range(2)
        ]
        both = jnp.concatenate(both, axis=1).astype(jnp.bfloat16)
        weighted_ref[:, wide] = both
        product = lax.dot_general(
            shifted[:, wide],
            both,
            (((1,), (1,)), ((), ())),
            preferred_element_type=jnp.float32,
        )
        total = product if total is None else total + product
    scores = scores_ref[0 : 9 * padded + 8] + total
    scores_ref[0 : 9 * padded + 8] = scores
    partial_ref[...] = jnp.broadcast_to(log_sum(scores)[None], partial_ref.shape)


def update_kernel(
    ngroups, partial_ref, scores_ref, weighted_ref, likelihood_ref, out_hbm, out_ref, sems
):
    orients = (out_ref.shape[1] - 8) // 2
    padded = (orients + 7) // 8 * 8
    width = out_ref.shape[2]
    stores = [
        pltpu.make_async_copy(out_ref.at[share], out_hbm.at[share], sems.at[share])
        for share in range(out_ref.shape[0])
    ]
    likelihood = log_sum(partial_ref[:, 0, :])
    likelihood_ref[...] = likelihood
    rows = 9 * padded + 8
    posterior = jnp.exp(scores_ref[0:rows] - likelihood).astype(jnp.bfloat16)
    group_hot = scores_ref[rows : rows + ngroups].astype(jnp.bfloat16)
    mass = lax.dot_general(
        posterior, group_hot, (((1,), (1,)), ((), ())), preferred_element_type=jnp.float32
    )
    group_mass = mass[0:padded]
    for k in range(8):
        group_mass += mass[48 + k * padded : 48 + (k + 1) * padded]
    pieces = [group_mass[r : r + 8] for r in range(0, padded, 8)]
    room = width - ngroups * len(pieces)
    mass_rows = jnp.concatenate(pieces + [jnp.zeros((8, room), jnp.float32)], axis=1)
    for share in range(out_ref.shape[0]):
        out_ref[share, 2 * orients :, :] = mass_rows
        for step in range(width // LANES):
            b = share * (width // LANES) + step
            table = rows + ngroups + 8 * b
            product = jnp.dot(
                posterior,
                weighted_ref[:, 2 * b * LANES : 2 * (b + 1) * LANES],
                preferred_element_type=jnp.float32,
            )
            real = product[0:padded, 0:LANES]
            imag = product[0:padded, LANES:]
            for k in range(4):
                cosine = scores_ref[table + k : table + k + 1, 0:LANES]
                sine = scores_ref[table + k + 4 : table + k + 5, 0:LANES]
                low = 48 + 2 * padded * k
                ahead = product[low : low + padded]
                behind = product[low + padded : low + 2 * padded]
                both, apart = ahead + behind, ahead - behind
                real += both[:, 0:LANES] * cosine - apart[:, LANES:] * sine
                imag += apart[:, 0:LANES] * sine + both[:, LANES:] * cosine
            there = slice(step * LANES, (step + 1) * LANES)
            out_ref[share, 0:orients, there] = real[0:orients]
            out_ref[share, orients : 2 * orients, there] = imag[0:orients]
        stores[share].start()
    for store in stores:
        store.wait()


def divide_kernel(share_ref, received_ref, noise_ref, out_ref):
    del share_ref
    rows = received_ref.shape[1]
    width = received_ref.shape[2]
    orients = (rows - 8) // 2
    padded = (orients + 7) // 8 * 8
    ngroups = noise_ref.shape[0]
    total = received_ref[0]
    for peer in range(1, received_ref.shape[0]):
        total += received_ref[peer]
    packed = total[2 * orients :]
    group_mass = jnp.concatenate(
        [packed[:, r * ngroups : (r + 1) * ngroups] for r in range(padded // 8)], axis=0
    )
    noise_mass = jnp.dot(
        group_mass, noise_ref[...], precision=HIGHEST, preferred_element_type=jnp.float32
    )
    scale = 1.0 / (noise_mass[0:orients] + RIDGE)
    for part in range(2):
        values = total[part * orients : (part + 1) * orients] * scale
        for b in range(width // LANES):
            out_ref[pl.ds(2 * b + part, orients, stride=2 * (width // LANES)), :] = values[
                :, b * LANES : (b + 1) * LANES
            ]


def rows_of(array):
    count, parts, coeffs = array.shape
    blocks = coeffs // LANES
    return (
        array.reshape(count, parts, blocks, LANES)
        .transpose(0, 2, 1, 3)
        .reshape(count * blocks * parts, LANES)
    )


def kernel_params(limit):
    return pltpu.CompilerParams(vmem_limit_bytes=limit)


def score_call(images, references, noise_weights, log_prior, groups, prior_index, class_map, phase, spread):
    particles, _, coeffs = images.shape
    orients = references.shape[0]
    padded = (orients + 7) // 8 * 8
    rows = 9 * padded + 8
    ngroups = noise_weights.shape[0]
    operands = [
        rows_of(images),
        rows_of(references),
        noise_weights,
        log_prior,
        groups,
        prior_index,
        class_map,
        phase,
    ]
    return pl.pallas_call(
        score_kernel,
        in_specs=[pl.BlockSpec(memory_space=pltpu.HBM)] * 8,
        out_specs=[pl.BlockSpec(memory_space=pltpu.VMEM)] * 3,
        out_shape=[
            pltpu.VMEM((rows + ngroups + 8 * coeffs // LANES, particles), jnp.float32),
            pltpu.VMEM((particles, 2 * coeffs), jnp.bfloat16),
            jax.ShapeDtypeStruct((spread, 1, particles), jnp.float32),
        ],
        scratch_shapes=[pltpu.VMEM(array.shape, array.dtype) for array in operands]
        + [
            pltpu.VMEM((particles * (2 * coeffs // LANES + 1), LANES), jnp.float32),
            pltpu.VMEM((padded * (2 * coeffs // LANES + 1), LANES), jnp.float32),
            pltpu.VMEM((rows, 2 * coeffs), jnp.bfloat16),
            pltpu.VMEM((particles, coeffs), jnp.float32),
            pltpu.VMEM((3 * padded, coeffs), jnp.bfloat16),
            pltpu.SemaphoreType.DMA((8,)),
        ],
        compiler_params=kernel_params(SCORE_VMEM),
        name="score",
    )(*[pltpu.with_memory_space_constraint(array, pltpu.HBM) for array in operands])


def update_call(partials, scores, weighted, ngroups, orients, shares):
    particles, wide = weighted.shape
    block = (shares, 2 * orients + 8, wide // 2 // shares)
    kept = [
        pltpu.with_memory_space_constraint(array, pltpu.VMEM)
        for array in (scores, weighted)
    ]
    whole = pl.BlockSpec(memory_space=pltpu.VMEM)

    return pl.pallas_call(
        functools.partial(update_kernel, ngroups),
        in_specs=[whole] * 3,
        out_specs=[whole, pl.BlockSpec(memory_space=pltpu.HBM)],
        out_shape=[
            jax.ShapeDtypeStruct((1, particles), jnp.float32),
            pltpu.HBM(block, jnp.float32),
        ],
        scratch_shapes=[pltpu.VMEM(block, jnp.float32), pltpu.SemaphoreType.DMA((shares,))],
        compiler_params=kernel_params(OTHER_VMEM),
        name="update",
    )(partials, *kept)


def divide_call(share, received, noise_weights):
    shares, rows, width = received.shape
    orients = (rows - 8) // 2
    ngroups = noise_weights.shape[0]
    return pl.pallas_call(
        divide_kernel,
        grid_spec=pltpu.PrefetchScalarGridSpec(
            num_scalar_prefetch=1,
            grid=(1,),
            in_specs=[
                pl.BlockSpec((shares, rows, width), lambda i, s: (0, 0, 0)),
                pl.BlockSpec((ngroups, width), lambda i, s: (0, s[0])),
            ],
            out_specs=pl.BlockSpec((orients * 2 * width // LANES, LANES), lambda i, s: (0, 0)),
        ),
        out_shape=jax.ShapeDtypeStruct((orients * 2 * width // LANES, LANES), jnp.float32),
        compiler_params=kernel_params(OTHER_VMEM),
        name="divide",
    )(
        share,
        pltpu.with_memory_space_constraint(received, pltpu.VMEM),
        pltpu.with_memory_space_constraint(noise_weights, pltpu.HBM),
    )


def exchange(spread, axes):
    return lax.all_to_all(spread, axes, 0, 0, tiled=True)


def shards(images, references, noise_weights, log_prior, groups, prior_index, class_map):
    coeffs = images.shape[2]
    orients = references.shape[0]
    phase = jnp.asarray(phase_tables(coeffs))
    depth = lax.axis_size("z")
    plane = lax.axis_size("x") * lax.axis_size("core")
    shares = lax.axis_size("dom")
    scores, weighted, partial = score_call(
        images, references, noise_weights, log_prior, groups, prior_index, class_map, phase, plane
    )
    partial = log_sum(exchange(partial, ("x", "core"))[:, 0, :])
    partial = jnp.broadcast_to(partial[None], (depth, 1, partial.shape[1]))
    partials = exchange(partial, "z")
    likelihood, blocks = update_call(
        partials, scores, weighted, noise_weights.shape[0], orients, shares
    )
    received = exchange(blocks, "dom")
    share = lax.axis_index("dom").astype(jnp.int32)[None]
    new_rows = divide_call(share, received, noise_weights)
    width = coeffs // shares
    new_references = (
        new_rows.reshape(orients, width // LANES, 2, LANES)
        .transpose(0, 2, 1, 3)
        .reshape(orients, 2, width)
    )
    return (new_references, likelihood[0])


def solution(mesh):
    fine = Mesh(mesh.devices.reshape(16, 4, 2, 4), ("z", "x", "core", "dom"))
    orient = ("z", "x", "core")
    in_specs = (
        P("dom", None, None),
        P(orient, None, None),
        P(),
        P(),
        P("dom"),
        P("dom"),
        P(orient),
    )
    out_specs = (P(orient, None, "dom"), P("dom"))
    return jax.shard_map(shards, mesh=fine, in_specs=in_specs, out_specs=out_specs, check_vma=False)
```

```python
import functools

import jax
import jax.numpy as jnp
import numpy as np
from jax import lax
from jax.experimental import pallas as pl
from jax.experimental.pallas import tpu as pltpu
from jax.sharding import Mesh
from jax.sharding import PartitionSpec as P

BOX = 64
RIDGE = 0.01
LANES = 128
PAIRS = (5, 6, 7, 8)
LOWEST = -1.0e30
HIGHEST = lax.Precision.HIGHEST
SCORE_VMEM = 36 * 1024 * 1024
OTHER_VMEM = 24 * 1024 * 1024


def phase_tables(coeffs):
    index = np.arange(coeffs)
    row = index // (BOX // 2)
    freq_y = (row + BOX // 2) % BOX - BOX // 2
    freq_x = index % (BOX // 2)
    shift = np.array(PAIRS)
    turns = (shift % 3 - 1)[:, None] * freq_x[None] + (shift // 3 - 1)[:, None] * freq_y[None]
    angle = (turns % BOX) * (2.0 * np.pi / BOX)
    return np.concatenate([np.cos(angle), np.sin(angle)]).astype(np.float32)


def split_bf16(values):
    high = values.astype(jnp.bfloat16)
    rest = values - high.astype(jnp.float32)
    mid = rest.astype(jnp.bfloat16)
    low = (rest - mid.astype(jnp.float32)).astype(jnp.bfloat16)
    return high, mid, low


def log_sum(rows):
    peak = jnp.max(rows, axis=0, keepdims=True)
    return peak + jnp.log(jnp.sum(jnp.exp(rows - peak), axis=0, keepdims=True))


def hot_columns(count, index_row):
    rows = lax.broadcasted_iota(jnp.int32, (count, index_row.shape[1]), 0)
    return rows == index_row


def score_kernel(
    images_hbm,
    refs_hbm,
    noise_hbm,
    prior_hbm,
    groups_hbm,
    prior_index_hbm,
    class_hbm,
    phase_hbm,
    scores_ref,
    weighted_ref,
    share_ref,
    partial_ref,
    images_ref,
    refs_ref,
    noise_ref,
    prior_ref,
    groups_ref,
    prior_index_ref,
    class_ref,
    phase_ref,
    image_wide,
    ref_wide,
    shifted,
    weights,
    power,
    sems,
):
    particles = groups_ref.shape[0]
    coeffs = noise_ref.shape[1]
    ngroups = noise_ref.shape[0]
    blocks = coeffs // LANES
    orients = class_ref.shape[0]
    padded = (orients + 7) // 8 * 8
    rows = 2 * blocks
    pitch = rows + 1
    pairs = (
        (refs_hbm, refs_ref),
        (phase_hbm, phase_ref),
        (groups_hbm, groups_ref),
        (noise_hbm, noise_ref),
        (prior_index_hbm, prior_index_ref),
        (class_hbm, class_ref),
        (prior_hbm, prior_ref),
        (images_hbm, images_ref),
    )
    fetches = [pltpu.make_async_copy(*pair, sems.at[i]) for i, pair in enumerate(pairs)]
    for fetch in fetches:
        fetch.start()
    for fetch in fetches[:3]:
        fetch.wait()
    tables = 9 * padded + 8 + ngroups
    for b in range(blocks):
        scores_ref[tables + 8 * b : tables + 8 * b + 8, 0:LANES] = phase_ref[
            :, b * LANES : (b + 1) * LANES
        ]

    def spread(source, target, first, count):
        for k in range(count):
            wide = source[pl.ds((first + k) * rows, rows), :].astype(jnp.float32)
            for step in range(0, rows, 8):
                target[pl.ds(pl.multiple_of(first * pitch, 8) + k * pitch + step, 8), :] = wide[
                    step : step + 8
                ]

    for first in range(0, orients, 8):
        spread(refs_ref, ref_wide, first, min(8, orients - first))
    ref_wide[orients * pitch :, :] = jnp.zeros(
        (ref_wide.shape[0] - orients * pitch, LANES), jnp.float32
    )
    group_hot = hot_columns(ngroups, groups_ref[...].reshape(1, particles))
    group_hot = group_hot.astype(jnp.float32)
    scores_ref[9 * padded + 8 : tables] = group_hot
    group_hot = group_hot.astype(jnp.bfloat16)
    fetches[3].wait()
    width = share_ref.shape[1]
    mine = pl.multiple_of(lax.axis_index("dom") * width, width)
    share_ref[...] = noise_ref[:, pl.ds(mine, width)]
    noise_parts = jnp.concatenate(split_bf16(noise_ref[...]), axis=0)
    weights[...] = lax.dot_general(
        jnp.concatenate([group_hot] * 3, axis=0),
        noise_parts,
        (((0,), (0,)), ((), ())),
        preferred_element_type=jnp.float32,
    )
    for b in range(blocks):
        here = pl.ds(b * LANES, LANES)
        real = ref_wide[pl.ds(2 * b, padded, stride=pitch), :]
        imag = ref_wide[pl.ds(2 * b + 1, padded, stride=pitch), :]
        power[:, here] = jnp.concatenate(split_bf16(real * real + imag * imag), axis=0)
        reals = [real, jnp.zeros((8, LANES), jnp.float32)]
        imags = [imag, jnp.zeros((8, LANES), jnp.float32)]
        for k in range(4):
            cosine = phase_ref[k : k + 1, here]
            sine = phase_ref[k + 4 : k + 5, here]
            real_cos, real_sin = real * cosine, real * sine
            imag_cos, imag_sin = imag * cosine, imag * sine
            reals += [real_cos + imag_sin, real_cos - imag_sin]
            imags += [imag_cos - real_sin, imag_cos + real_sin]
        wide = b * 2 * LANES
        shifted[:, pl.ds(wide, LANES)] = jnp.concatenate(reals, axis=0).astype(jnp.bfloat16)
        shifted[:, pl.ds(wide + LANES, LANES)] = jnp.concatenate(imags, axis=0).astype(
            jnp.bfloat16
        )

    products = lax.dot_general(
        power[...], noise_parts, (((1,), (1,)), ((), ())), preferred_element_type=jnp.float32
    )
    products = products[0:padded] + products[padded : 2 * padded] + products[2 * padded :]
    quadratic = (
        products[:, 0:ngroups]
        + products[:, ngroups : 2 * ngroups]
        + products[:, 2 * ngroups : 3 * ngroups]
    )
    for fetch in fetches[4:7]:
        fetch.wait()
    class_hot = hot_columns(prior_ref.shape[1], class_ref[...].reshape(1, orients))
    class_prior = lax.dot_general(
        class_hot.astype(jnp.float32),
        prior_ref[...],
        (((0,), (1,)), ((), ())),
        precision=HIGHEST,
        preferred_element_type=jnp.float32,
    )
    class_prior = jnp.concatenate(
        [class_prior, jnp.zeros((padded - orients, prior_ref.shape[0]), jnp.float32)], axis=0
    )
    prior_hot = hot_columns(prior_ref.shape[0], prior_index_ref[...].reshape(1, particles))
    prior_hot = prior_hot.astype(jnp.float32)
    offsets = jnp.dot(
        jnp.concatenate(split_bf16(-0.5 * quadratic), axis=1),
        jnp.concatenate([group_hot] * 3, axis=0),
        preferred_element_type=jnp.float32,
    ) + jnp.dot(class_prior, prior_hot, precision=HIGHEST, preferred_element_type=jnp.float32)
    real_row = lax.broadcasted_iota(jnp.int32, (padded, particles), 0) < orients
    offsets = jnp.where(real_row, offsets, LOWEST)

    scores_ref[0 : 9 * padded + 8] = jnp.concatenate(
        [offsets, jnp.full((8, particles), LOWEST, jnp.float32)] + [offsets] * 8, axis=0
    )
    fetches[7].wait()

    @pl.loop(0, particles // 32)
    def _(g):
        for h in range(4):
            spread(images_ref, image_wide, g * 32 + h * 8, 8)

    total = None
    for b in range(blocks):
        weight = weights[:, pl.ds(b * LANES, LANES)]
        wide = pl.ds(b * 2 * LANES, 2 * LANES)
        both = [
            image_wide[pl.ds(2 * b + part, particles, stride=pitch), :] * weight
            for part in range(2)
        ]
        both = jnp.concatenate(both, axis=1).astype(jnp.bfloat16)
        weighted_ref[:, wide] = both
        product = lax.dot_general(
            shifted[:, wide],
            both,
            (((1,), (1,)), ((), ())),
            preferred_element_type=jnp.float32,
        )
        total = product if total is None else total + product
    scores = scores_ref[0 : 9 * padded + 8] + total
    scores_ref[0 : 9 * padded + 8] = scores
    partial_ref[...] = jnp.broadcast_to(log_sum(scores)[None], partial_ref.shape)


def update_kernel(
    ngroups, partial_ref, scores_ref, weighted_ref, likelihood_ref, out_ref
):
    orients = (out_ref.shape[1] - 8) // 2
    padded = (orients + 7) // 8 * 8
    width = out_ref.shape[2]
    likelihood = log_sum(partial_ref[:, 0, :])
    likelihood_ref[...] = likelihood
    rows = 9 * padded + 8
    posterior = jnp.exp(scores_ref[0:rows] - likelihood).astype(jnp.bfloat16)
    group_hot = scores_ref[rows : rows + ngroups].astype(jnp.bfloat16)
    mass = lax.dot_general(
        posterior, group_hot, (((1,), (1,)), ((), ())), preferred_element_type=jnp.float32
    )
    group_mass = mass[0:padded]
    for k in range(8):
        group_mass += mass[48 + k * padded : 48 + (k + 1) * padded]
    pieces = [group_mass[r : r + 8] for r in range(0, padded, 8)]
    room = width - ngroups * len(pieces)
    mass_rows = jnp.concatenate(pieces + [jnp.zeros((8, room), jnp.float32)], axis=1)
    for share in range(out_ref.shape[0]):
        out_ref[share, 2 * orients :, :] = mass_rows
        for step in range(width // LANES):
            b = share * (width // LANES) + step
            table = rows + ngroups + 8 * b
            product = jnp.dot(
                posterior,
                weighted_ref[:, 2 * b * LANES : 2 * (b + 1) * LANES],
                preferred_element_type=jnp.float32,
            )
            real = product[0:padded, 0:LANES]
            imag = product[0:padded, LANES:]
            for k in range(4):
                cosine = scores_ref[table + k : table + k + 1, 0:LANES]
                sine = scores_ref[table + k + 4 : table + k + 5, 0:LANES]
                low = 48 + 2 * padded * k
                ahead = product[low : low + padded]
                behind = product[low + padded : low + 2 * padded]
                both, apart = ahead + behind, ahead - behind
                real += both[:, 0:LANES] * cosine - apart[:, LANES:] * sine
                imag += apart[:, 0:LANES] * sine + both[:, LANES:] * cosine
            there = slice(step * LANES, (step + 1) * LANES)
            out_ref[share, 0:orients, there] = real[0:orients]
            out_ref[share, orients : 2 * orients, there] = imag[0:orients]


def divide_kernel(received_ref, noise_ref, likelihood_ref, out_ref, likelihood_out):
    likelihood_out[...] = likelihood_ref[...].reshape(likelihood_out.shape)
    rows = received_ref.shape[1]
    width = received_ref.shape[2]
    orients = (rows - 8) // 2
    padded = (orients + 7) // 8 * 8
    ngroups = noise_ref.shape[0]
    total = received_ref[0]
    for peer in range(1, received_ref.shape[0]):
        total += received_ref[peer]
    packed = total[2 * orients :]
    group_mass = jnp.concatenate(
        [packed[:, r * ngroups : (r + 1) * ngroups] for r in range(padded // 8)], axis=0
    )
    noise_mass = jnp.dot(
        group_mass, noise_ref[...], precision=HIGHEST, preferred_element_type=jnp.float32
    )
    scale = 1.0 / (noise_mass[0:orients] + RIDGE)
    for part in range(2):
        values = total[part * orients : (part + 1) * orients] * scale
        for b in range(width // LANES):
            out_ref[pl.ds(2 * b + part, orients, stride=2 * (width // LANES)), :] = values[
                :, b * LANES : (b + 1) * LANES
            ]


def rows_of(array):
    count, parts, coeffs = array.shape
    blocks = coeffs // LANES
    return (
        array.reshape(count, parts, blocks, LANES)
        .transpose(0, 2, 1, 3)
        .reshape(count * blocks * parts, LANES)
    )


def kernel_params(limit):
    return pltpu.CompilerParams(vmem_limit_bytes=limit)


def score_call(images, references, noise_weights, log_prior, groups, prior_index, class_map, phase, spread, shares):
    particles, _, coeffs = images.shape
    orients = references.shape[0]
    padded = (orients + 7) // 8 * 8
    rows = 9 * padded + 8
    ngroups = noise_weights.shape[0]
    operands = [
        rows_of(images),
        rows_of(references),
        noise_weights,
        log_prior,
        groups,
        prior_index,
        class_map,
        phase,
    ]
    return pl.pallas_call(
        score_kernel,
        in_specs=[pl.BlockSpec(memory_space=pltpu.HBM)] * 8,
        out_specs=[pl.BlockSpec(memory_space=pltpu.VMEM)] * 4,
        out_shape=[
            pltpu.VMEM((rows + ngroups + 8 * coeffs // LANES, particles), jnp.float32),
            pltpu.VMEM((particles, 2 * coeffs), jnp.bfloat16),
            pltpu.VMEM((ngroups, coeffs // shares), jnp.float32),
            jax.ShapeDtypeStruct((spread, 1, particles), jnp.float32),
        ],
        scratch_shapes=[pltpu.VMEM(array.shape, array.dtype) for array in operands]
        + [
            pltpu.VMEM((particles * (2 * coeffs // LANES + 1), LANES), jnp.float32),
            pltpu.VMEM((padded * (2 * coeffs // LANES + 1), LANES), jnp.float32),
            pltpu.VMEM((rows, 2 * coeffs), jnp.bfloat16),
            pltpu.VMEM((particles, coeffs), jnp.float32),
            pltpu.VMEM((3 * padded, coeffs), jnp.bfloat16),
            pltpu.SemaphoreType.DMA((8,)),
        ],
        compiler_params=kernel_params(SCORE_VMEM),
        name="score",
    )(*[pltpu.with_memory_space_constraint(array, pltpu.HBM) for array in operands])


def update_call(partials, scores, weighted, ngroups, orients, shares):
    particles, wide = weighted.shape
    block = (shares, 2 * orients + 8, wide // 2 // shares)
    kept = [
        pltpu.with_memory_space_constraint(array, pltpu.VMEM)
        for array in (scores, weighted)
    ]
    whole = pl.BlockSpec(memory_space=pltpu.VMEM)

    return pl.pallas_call(
        functools.partial(update_kernel, ngroups),
        in_specs=[whole] * 3,
        out_specs=[whole] * 2,
        out_shape=[
            pltpu.VMEM((1, particles), jnp.float32),
            pltpu.VMEM(block, jnp.float32),
        ],
        compiler_params=kernel_params(OTHER_VMEM),
        name="update",
    )(partials, *kept)


def divide_call(received, noise_share, likelihood):
    shares, rows, width = received.shape
    orients = (rows - 8) // 2
    operands = [
        pltpu.with_memory_space_constraint(array, pltpu.VMEM)
        for array in (received, noise_share, likelihood)
    ]
    return pl.pallas_call(
        divide_kernel,
        in_specs=[pl.BlockSpec(memory_space=pltpu.VMEM)] * 3,
        out_specs=[pl.BlockSpec(memory_space=pltpu.VMEM)] * 2,
        out_shape=[
            jax.ShapeDtypeStruct((orients * 2 * width // LANES, LANES), jnp.float32),
            jax.ShapeDtypeStruct(likelihood.shape[1:], jnp.float32),
        ],
        compiler_params=kernel_params(OTHER_VMEM),
        name="divide",
    )(*operands)


def exchange(spread, axes):
    return lax.all_to_all(spread, axes, 0, 0, tiled=True)


def shards(images, references, noise_weights, log_prior, groups, prior_index, class_map):
    coeffs = images.shape[2]
    orients = references.shape[0]
    phase = jnp.asarray(phase_tables(coeffs))
    depth = lax.axis_size("z")
    plane = lax.axis_size("x") * lax.axis_size("core")
    shares = lax.axis_size("dom")
    scores, weighted, noise_share, partial = score_call(
        images, references, noise_weights, log_prior, groups, prior_index, class_map, phase, plane, shares
    )
    partial = log_sum(exchange(partial, ("x", "core"))[:, 0, :])
    partial = jnp.broadcast_to(partial[None], (depth, 1, partial.shape[1]))
    partials = exchange(partial, "z")
    likelihood, blocks = update_call(
        partials, scores, weighted, noise_weights.shape[0], orients, shares
    )
    received = exchange(blocks, "dom")
    new_rows, likelihood = divide_call(received, noise_share, likelihood)
    width = coeffs // shares
    new_references = (
        new_rows.reshape(orients, width // LANES, 2, LANES)
        .transpose(0, 2, 1, 3)
        .reshape(orients, 2, width)
    )
    return (new_references, likelihood)


def solution(mesh):
    fine = Mesh(mesh.devices.reshape(16, 4, 2, 4), ("z", "x", "core", "dom"))
    orient = ("z", "x", "core")
    in_specs = (
        P("dom", None, None),
        P(orient, None, None),
        P(),
        P(),
        P("dom"),
        P("dom"),
        P(orient),
    )
    out_specs = (P(orient, None, "dom"), P("dom"))
    return jax.shard_map(shards, mesh=fine, in_specs=in_specs, out_specs=out_specs, check_vma=False)
```

```python
import functools

import jax
import jax.numpy as jnp
import numpy as np
from jax import lax
from jax.experimental import pallas as pl
from jax.experimental.pallas import tpu as pltpu
from jax.sharding import Mesh
from jax.sharding import PartitionSpec as P

BOX = 64
RIDGE = 0.01
LANES = 128
PAIRS = (5, 6, 7, 8)
LOWEST = -1.0e30
HIGHEST = lax.Precision.HIGHEST
SCORE_VMEM = 36 * 1024 * 1024
OTHER_VMEM = 24 * 1024 * 1024


def phase_tables(coeffs):
    index = np.arange(coeffs)
    row = index // (BOX // 2)
    freq_y = (row + BOX // 2) % BOX - BOX // 2
    freq_x = index % (BOX // 2)
    shift = np.array(PAIRS)
    turns = (shift % 3 - 1)[:, None] * freq_x[None] + (shift // 3 - 1)[:, None] * freq_y[None]
    angle = (turns % BOX) * (2.0 * np.pi / BOX)
    return np.concatenate([np.cos(angle), np.sin(angle)]).astype(np.float32)


def split_bf16(values):
    high = values.astype(jnp.bfloat16)
    rest = values - high.astype(jnp.float32)
    mid = rest.astype(jnp.bfloat16)
    low = (rest - mid.astype(jnp.float32)).astype(jnp.bfloat16)
    return high, mid, low


def log_sum(rows):
    peak = jnp.max(rows, axis=0, keepdims=True)
    return peak + jnp.log(jnp.sum(jnp.exp(rows - peak), axis=0, keepdims=True))


def hot_columns(count, index_row):
    rows = lax.broadcasted_iota(jnp.int32, (count, index_row.shape[1]), 0)
    return rows == index_row


def score_kernel(
    images_hbm,
    refs_hbm,
    noise_hbm,
    prior_hbm,
    groups_hbm,
    prior_index_hbm,
    class_hbm,
    phase_hbm,
    scores_ref,
    weighted_ref,
    share_ref,
    partial_ref,
    images_ref,
    refs_ref,
    noise_ref,
    prior_ref,
    groups_ref,
    prior_index_ref,
    class_ref,
    phase_ref,
    image_wide,
    ref_wide,
    shifted,
    weights,
    power,
    sems,
):
    particles = groups_ref.shape[0]
    coeffs = noise_ref.shape[1]
    ngroups = noise_ref.shape[0]
    blocks = coeffs // LANES
    orients = class_ref.shape[0]
    padded = (orients + 7) // 8 * 8
    rows = 2 * blocks
    pitch = rows + 1
    pairs = (
        (refs_hbm, refs_ref),
        (phase_hbm, phase_ref),
        (groups_hbm, groups_ref),
        (noise_hbm, noise_ref),
        (prior_index_hbm, prior_index_ref),
        (class_hbm, class_ref),
        (prior_hbm, prior_ref),
        (images_hbm, images_ref),
    )
    fetches = [pltpu.make_async_copy(*pair, sems.at[i]) for i, pair in enumerate(pairs)]
    for fetch in fetches:
        fetch.start()
    for fetch in fetches[:3]:
        fetch.wait()
    tables = 9 * padded + 8 + ngroups
    for b in range(blocks):
        scores_ref[tables + 8 * b : tables + 8 * b + 8, 0:LANES] = phase_ref[
            :, b * LANES : (b + 1) * LANES
        ]

    def spread(source, target, first, count):
        for k in range(count):
            wide = source[pl.ds((first + k) * rows, rows), :].astype(jnp.float32)
            for step in range(0, rows, 8):
                target[pl.ds(pl.multiple_of(first * pitch, 8) + k * pitch + step, 8), :] = wide[
                    step : step + 8
                ]

    for first in range(0, orients, 8):
        spread(refs_ref, ref_wide, first, min(8, orients - first))
    ref_wide[orients * pitch :, :] = jnp.zeros(
        (ref_wide.shape[0] - orients * pitch, LANES), jnp.float32
    )
    group_hot = hot_columns(ngroups, groups_ref[...].reshape(1, particles))
    group_hot = group_hot.astype(jnp.float32)
    scores_ref[9 * padded + 8 : tables] = group_hot
    group_hot = group_hot.astype(jnp.bfloat16)
    fetches[3].wait()
    width = share_ref.shape[1]
    mine = pl.multiple_of(lax.axis_index("dom") * width, width)
    share_ref[...] = noise_ref[:, pl.ds(mine, width)]
    noise_parts = jnp.concatenate(split_bf16(noise_ref[...]), axis=0)
    weights[...] = lax.dot_general(
        jnp.concatenate([group_hot] * 3, axis=0),
        noise_parts,
        (((0,), (0,)), ((), ())),
        preferred_element_type=jnp.float32,
    )
    for b in range(blocks):
        here = pl.ds(b * LANES, LANES)
        real = ref_wide[pl.ds(2 * b, padded, stride=pitch), :]
        imag = ref_wide[pl.ds(2 * b + 1, padded, stride=pitch), :]
        power[:, here] = jnp.concatenate(split_bf16(real * real + imag * imag), axis=0)
        reals = [real, jnp.zeros((8, LANES), jnp.float32)]
        imags = [imag, jnp.zeros((8, LANES), jnp.float32)]
        for k in range(4):
            cosine = phase_ref[k : k + 1, here]
            sine = phase_ref[k + 4 : k + 5, here]
            real_cos, real_sin = real * cosine, real * sine
            imag_cos, imag_sin = imag * cosine, imag * sine
            reals += [real_cos + imag_sin, real_cos - imag_sin]
            imags += [imag_cos - real_sin, imag_cos + real_sin]
        wide = b * 2 * LANES
        shifted[:, pl.ds(wide, LANES)] = jnp.concatenate(reals, axis=0).astype(jnp.bfloat16)
        shifted[:, pl.ds(wide + LANES, LANES)] = jnp.concatenate(imags, axis=0).astype(
            jnp.bfloat16
        )

    products = lax.dot_general(
        power[...], noise_parts, (((1,), (1,)), ((), ())), preferred_element_type=jnp.float32
    )
    products = products[0:padded] + products[padded : 2 * padded] + products[2 * padded :]
    quadratic = (
        products[:, 0:ngroups]
        + products[:, ngroups : 2 * ngroups]
        + products[:, 2 * ngroups : 3 * ngroups]
    )
    for fetch in fetches[4:7]:
        fetch.wait()
    class_hot = hot_columns(prior_ref.shape[1], class_ref[...].reshape(1, orients))
    class_prior = lax.dot_general(
        class_hot.astype(jnp.float32),
        prior_ref[...],
        (((0,), (1,)), ((), ())),
        precision=HIGHEST,
        preferred_element_type=jnp.float32,
    )
    class_prior = jnp.concatenate(
        [class_prior, jnp.zeros((padded - orients, prior_ref.shape[0]), jnp.float32)], axis=0
    )
    prior_hot = hot_columns(prior_ref.shape[0], prior_index_ref[...].reshape(1, particles))
    prior_hot = prior_hot.astype(jnp.float32)
    offsets = jnp.dot(
        jnp.concatenate(split_bf16(-0.5 * quadratic), axis=1),
        jnp.concatenate([group_hot] * 3, axis=0),
        preferred_element_type=jnp.float32,
    ) + jnp.dot(class_prior, prior_hot, precision=HIGHEST, preferred_element_type=jnp.float32)
    real_row = lax.broadcasted_iota(jnp.int32, (padded, particles), 0) < orients
    offsets = jnp.where(real_row, offsets, LOWEST)

    scores_ref[0 : 9 * padded + 8] = jnp.concatenate(
        [offsets, jnp.full((8, particles), LOWEST, jnp.float32)] + [offsets] * 8, axis=0
    )
    fetches[7].wait()

    @pl.loop(0, particles // 144)
    def _(g):
        for h in range(18):
            spread(images_ref, image_wide, g * 144 + h * 8, 8)

    total = None
    for b in range(blocks):
        weight = weights[:, pl.ds(b * LANES, LANES)]
        wide = pl.ds(b * 2 * LANES, 2 * LANES)
        both = [
            image_wide[pl.ds(2 * b + part, particles, stride=pitch), :] * weight
            for part in range(2)
        ]
        both = jnp.concatenate(both, axis=1).astype(jnp.bfloat16)
        weighted_ref[:, wide] = both
        product = lax.dot_general(
            shifted[:, wide],
            both,
            (((1,), (1,)), ((), ())),
            preferred_element_type=jnp.float32,
        )
        total = product if total is None else total + product
    scores = scores_ref[0 : 9 * padded + 8] + total
    scores_ref[0 : 9 * padded + 8] = scores
    partial_ref[...] = jnp.broadcast_to(log_sum(scores)[None], partial_ref.shape)


def update_kernel(
    ngroups, partial_ref, scores_ref, weighted_ref, likelihood_ref, out_ref
):
    orients = (out_ref.shape[1] - 8) // 2
    padded = (orients + 7) // 8 * 8
    width = out_ref.shape[2]
    likelihood = log_sum(partial_ref[:, 0, :])
    likelihood_ref[...] = likelihood
    rows = 9 * padded + 8
    posterior = jnp.exp(scores_ref[0:rows] - likelihood).astype(jnp.bfloat16)
    group_hot = scores_ref[rows : rows + ngroups].astype(jnp.bfloat16)
    mass = lax.dot_general(
        posterior, group_hot, (((1,), (1,)), ((), ())), preferred_element_type=jnp.float32
    )
    group_mass = mass[0:padded]
    for k in range(8):
        group_mass += mass[48 + k * padded : 48 + (k + 1) * padded]
    pieces = [group_mass[r : r + 8] for r in range(0, padded, 8)]
    room = width - ngroups * len(pieces)
    mass_rows = jnp.concatenate(pieces + [jnp.zeros((8, room), jnp.float32)], axis=1)
    for share in range(out_ref.shape[0]):
        out_ref[share, 2 * orients :, :] = mass_rows
        for step in range(width // LANES):
            b = share * (width // LANES) + step
            table = rows + ngroups + 8 * b
            product = jnp.dot(
                posterior,
                weighted_ref[:, 2 * b * LANES : 2 * (b + 1) * LANES],
                preferred_element_type=jnp.float32,
            )
            real = product[0:padded, 0:LANES]
            imag = product[0:padded, LANES:]
            for k in range(4):
                cosine = scores_ref[table + k : table + k + 1, 0:LANES]
                sine = scores_ref[table + k + 4 : table + k + 5, 0:LANES]
                low = 48 + 2 * padded * k
                ahead = product[low : low + padded]
                behind = product[low + padded : low + 2 * padded]
                both, apart = ahead + behind, ahead - behind
                real += both[:, 0:LANES] * cosine - apart[:, LANES:] * sine
                imag += apart[:, 0:LANES] * sine + both[:, LANES:] * cosine
            there = slice(step * LANES, (step + 1) * LANES)
            out_ref[share, 0:orients, there] = real[0:orients]
            out_ref[share, orients : 2 * orients, there] = imag[0:orients]


def divide_kernel(received_ref, noise_ref, likelihood_ref, out_ref, likelihood_out):
    likelihood_out[...] = likelihood_ref[...].reshape(likelihood_out.shape)
    rows = received_ref.shape[1]
    width = received_ref.shape[2]
    orients = (rows - 8) // 2
    padded = (orients + 7) // 8 * 8
    ngroups = noise_ref.shape[0]
    total = received_ref[0]
    for peer in range(1, received_ref.shape[0]):
        total += received_ref[peer]
    packed = total[2 * orients :]
    group_mass = jnp.concatenate(
        [packed[:, r * ngroups : (r + 1) * ngroups] for r in range(padded // 8)], axis=0
    )
    noise_mass = jnp.dot(
        group_mass, noise_ref[...], precision=HIGHEST, preferred_element_type=jnp.float32
    )
    scale = 1.0 / (noise_mass[0:orients] + RIDGE)
    for part in range(2):
        values = total[part * orients : (part + 1) * orients] * scale
        for b in range(width // LANES):
            out_ref[pl.ds(2 * b + part, orients, stride=2 * (width // LANES)), :] = values[
                :, b * LANES : (b + 1) * LANES
            ]


def rows_of(array):
    count, parts, coeffs = array.shape
    blocks = coeffs // LANES
    return (
        array.reshape(count, parts, blocks, LANES)
        .transpose(0, 2, 1, 3)
        .reshape(count * blocks * parts, LANES)
    )


def kernel_params(limit):
    return pltpu.CompilerParams(vmem_limit_bytes=limit)


def score_call(images, references, noise_weights, log_prior, groups, prior_index, class_map, phase, spread, shares):
    particles, _, coeffs = images.shape
    orients = references.shape[0]
    padded = (orients + 7) // 8 * 8
    rows = 9 * padded + 8
    ngroups = noise_weights.shape[0]
    operands = [
        rows_of(images),
        rows_of(references),
        noise_weights,
        log_prior,
        groups,
        prior_index,
        class_map,
        phase,
    ]
    return pl.pallas_call(
        score_kernel,
        in_specs=[pl.BlockSpec(memory_space=pltpu.HBM)] * 8,
        out_specs=[pl.BlockSpec(memory_space=pltpu.VMEM)] * 4,
        out_shape=[
            pltpu.VMEM((rows + ngroups + 8 * coeffs // LANES, particles), jnp.float32),
            pltpu.VMEM((particles, 2 * coeffs), jnp.bfloat16),
            pltpu.VMEM((ngroups, coeffs // shares), jnp.float32),
            jax.ShapeDtypeStruct((spread, 1, particles), jnp.float32),
        ],
        scratch_shapes=[pltpu.VMEM(array.shape, array.dtype) for array in operands]
        + [
            pltpu.VMEM((particles * (2 * coeffs // LANES + 1), LANES), jnp.float32),
            pltpu.VMEM((padded * (2 * coeffs // LANES + 1), LANES), jnp.float32),
            pltpu.VMEM((rows, 2 * coeffs), jnp.bfloat16),
            pltpu.VMEM((particles, coeffs), jnp.float32),
            pltpu.VMEM((3 * padded, coeffs), jnp.bfloat16),
            pltpu.SemaphoreType.DMA((8,)),
        ],
        compiler_params=kernel_params(SCORE_VMEM),
        name="score",
    )(*[pltpu.with_memory_space_constraint(array, pltpu.HBM) for array in operands])


def update_call(partials, scores, weighted, ngroups, orients, shares):
    particles, wide = weighted.shape
    block = (shares, 2 * orients + 8, wide // 2 // shares)
    kept = [
        pltpu.with_memory_space_constraint(array, pltpu.VMEM)
        for array in (scores, weighted)
    ]
    whole = pl.BlockSpec(memory_space=pltpu.VMEM)

    return pl.pallas_call(
        functools.partial(update_kernel, ngroups),
        in_specs=[whole] * 3,
        out_specs=[whole] * 2,
        out_shape=[
            pltpu.VMEM((1, particles), jnp.float32),
            pltpu.VMEM(block, jnp.float32),
        ],
        compiler_params=kernel_params(OTHER_VMEM),
        name="update",
    )(partials, *kept)


def divide_call(received, noise_share, likelihood):
    shares, rows, width = received.shape
    orients = (rows - 8) // 2
    operands = [
        pltpu.with_memory_space_constraint(array, pltpu.VMEM)
        for array in (received, noise_share, likelihood)
    ]
    return pl.pallas_call(
        divide_kernel,
        in_specs=[pl.BlockSpec(memory_space=pltpu.VMEM)] * 3,
        out_specs=[pl.BlockSpec(memory_space=pltpu.VMEM)] * 2,
        out_shape=[
            jax.ShapeDtypeStruct((orients * 2 * width // LANES, LANES), jnp.float32),
            jax.ShapeDtypeStruct(likelihood.shape[1:], jnp.float32),
        ],
        compiler_params=kernel_params(OTHER_VMEM),
        name="divide",
    )(*operands)


def exchange(spread, axes):
    return lax.all_to_all(spread, axes, 0, 0, tiled=True)


def shards(images, references, noise_weights, log_prior, groups, prior_index, class_map):
    coeffs = images.shape[2]
    orients = references.shape[0]
    phase = jnp.asarray(phase_tables(coeffs))
    depth = lax.axis_size("z")
    plane = lax.axis_size("x") * lax.axis_size("core")
    shares = lax.axis_size("dom")
    scores, weighted, noise_share, partial = score_call(
        images, references, noise_weights, log_prior, groups, prior_index, class_map, phase, plane, shares
    )
    partial = log_sum(exchange(partial, ("x", "core"))[:, 0, :])
    partial = jnp.broadcast_to(partial[None], (depth, 1, partial.shape[1]))
    partials = exchange(partial, "z")
    likelihood, blocks = update_call(
        partials, scores, weighted, noise_weights.shape[0], orients, shares
    )
    received = exchange(blocks, "dom")
    new_rows, likelihood = divide_call(received, noise_share, likelihood)
    width = coeffs // shares
    new_references = (
        new_rows.reshape(orients, width // LANES, 2, LANES)
        .transpose(0, 2, 1, 3)
        .reshape(orients, 2, width)
    )
    return (new_references, likelihood)


def solution(mesh):
    fine = Mesh(mesh.devices.reshape(16, 4, 2, 4), ("z", "x", "core", "dom"))
    orient = ("z", "x", "core")
    in_specs = (
        P("dom", None, None),
        P(orient, None, None),
        P(),
        P(),
        P("dom"),
        P("dom"),
        P(orient),
    )
    out_specs = (P(orient, None, "dom"), P("dom"))
    return jax.shard_map(shards, mesh=fine, in_specs=in_specs, out_specs=out_specs, check_vma=False)
```
